32 devices in a mesh: slab: 16 (over z, x, core), dp: 2 (over y).
Axes of the slice: x: 2, y: 2, z: 4, core: 2. Of those that a mesh axis runs over, the one named last changes fastest.
Arguments:
- point_feats: float32 [2, 8192, 128], P('dp', 'slab'), may hold values from -6 to 6
- owner_slab: int32 [2, 8192, 1], P('dp', 'slab'), may hold values from 0 to 15; in each aligned block of 512 rows (0 to 511, 512 to 1023, ..., all dimensions but the last counted through in order) at most 64 rows name the same one
- block_slot: int32 [2, 8192], P('dp', 'slab'), may hold values from 0 to 1
- voxel_index: int32 [2, 8192], P('dp', 'slab'), may hold values from 0 to 511
- boundary: int32 [2, 16, 2, 1], P('dp', 'slab'), may hold values from 0 to 1, as said below
- neighbours: int32 [2, 32, 27], P('dp', 'slab'), may hold values from 0 to 4, as said below
- weight_taps: float32 [27, 128, 128], replicated, may hold values from -0.109375 to 0.109375
- cotangent: float32 [2, 16384, 128], P('dp', 'slab'), may hold values from -6 to 6
Outputs:
- activated: float32 [2, 16384, 128], P('dp', 'slab')
- point_grads: float32 [2, 8192, 128], P('dp', 'slab')
- weight_grads: float32 [3456, 128], P('slab')
The draws below stay inside these ranges and needn't reach their ends.
Inputs may be any that keep to these rules, and one draw needn't show every extreme that they name: `owner_slab`: among the points of one device, no slab is named by more than 64 points, and exactly 64 in some device. `boundary`: each list of one slab holds 1 different block slots. `neighbours`: entry 13 of a block's row is the block's own slot. Entries 0 to 8 name a block of the slab (below 2), one of the 1 block from the slab before (2 to 2), or the zero block 4; entries 18 to 26 a block of the slab, one of the 1 block from the slab after, or the zero block; the others a block of the slab or the zero block.
All inputs are finite; a program needn't handle non-finite values.
Results may differ from the reference program's by a relative error of at most 0.0003.
Values sent between devices are 32-bit elements; how exact they have to be, the bound alone decides.
No kernel may reach another device: no remote copies, remote signals or barrier semaphores. Data moves between devices by JAX's collectives and lax.ppermute only.
A program may use at most 64 MiB of HBM per device.

```python
import math
import jax
import jax.numpy as jnp
import numpy as np
from jax import lax

C = 128
E = 8
NB = 2
NH = 1
P_DEV = 512
VOX = 512
CAP = 64
WIN = 2
N_SLAB = 16


def draw_boundary(key, part):
    subkeys = jax.random.split(jax.random.fold_in(key, 11), WIN * N_SLAB * 2)
    chosen = jax.vmap(lambda subkey: jax.random.permutation(subkey, NB)[:NH])(subkeys)
    return chosen.reshape(WIN, N_SLAB, 2, NH).astype(jnp.int32)


def draw_neighbours(key, part):
    raw_values = jax.random.randint(jax.random.fold_in(key, 7), (WIN, N_SLAB * NB, 27), 0, NB + NH + 1)
    column = jnp.arange(27)[None, None, :]
    offset_x = column // 9
    empty_slot = NB + 2 * NH
    lower = jnp.where(raw_values < NB + NH, raw_values, empty_slot)
    upper = jnp.where(raw_values < NB, raw_values, jnp.where(raw_values < NB + NH, raw_values + NH, empty_slot))
    middle = jnp.where(raw_values < NB, raw_values, empty_slot)
    chosen = jnp.where(offset_x == 0, lower, jnp.where(offset_x == 2, upper, middle))
    own_slot = (jnp.arange(N_SLAB * NB) % NB)[None, :, None]
    chosen = jnp.where(column == 13, own_slot, chosen)
    return chosen.astype(jnp.int32)


def touch_ends(entries, own_key, least, largest):
    longest = entries.shape.index(max(entries.shape))
    spots = []
    for shift in (0, 1):
        where = [jax.random.randint(jax.random.fold_in(own_key, axis), (), 0, length) for axis, length in enumerate(entries.shape)]
        where[longest] = (where[longest] + shift) % entries.shape[longest]
        spots.append(tuple(where))
    return entries.at[spots[0]].set(least).at[spots[1]].set(largest)


def steps_of(rng, dims, cuts, low, largest):
    loudness = 1.0
    for dim, shards_of in cuts:
        heights = jax.random.uniform(jax.random.fold_in(jax.random.fold_in(rng, 6), dim), (shards_of,), jnp.float32, low / len(cuts), largest / len(cuts))
        loudness = loudness * jnp.repeat(jnp.exp(heights), dims[dim] // shards_of).reshape((-1,) + (1,) * (len(dims) - 1 - dim))
    return loudness


def deal_out(stream_key, own, number, rows, amount, top, bound, skew):
    sequence = jax.random.permutation(stream_key, amount)
    packed, usual = shares(amount, rows * top, bound, skew, True), shares(amount, rows * top, bound, skew, False)
    places = jnp.arange(amount)

    def named(tallies, offset_by):
        used = int((tallies > 0).sum())
        fixed = max(1, used // 4)
        passed = fixed + (places - fixed + offset_by * (used - fixed)) % max(1, amount - fixed)
        return jnp.zeros((amount,), jnp.int32).at[sequence[jnp.where(places < fixed, places, passed)]].set(jnp.asarray(tallies, jnp.int32))

    tallies = jnp.where(number % 4 == 0, named(packed, number // 4), named(usual, number - number // 4 - 1))
    mixed = jax.random.permutation(jax.random.fold_in(own, 3), amount)
    source_of, receiver = mixed[0:amount // 2 * 2:2], mixed[1:amount // 2 * 2:2]
    margin = jnp.minimum(tallies[source_of] - 1, bound - tallies[receiver]) // 2
    margin = jnp.where((source_of == sequence[0]) | (receiver == sequence[0]) | (tallies[receiver] == 0), 0, jnp.maximum(margin, 0))
    passed = jax.random.randint(jax.random.fold_in(own, 4), (amount // 2,), 0, 1 << 20) % (margin + 1)
    tallies = tallies.at[source_of].add(-passed).at[receiver].add(passed)
    members = jnp.searchsorted(jnp.cumsum(tallies), jnp.arange(rows * top), side="right").astype(jnp.int32)
    table = members.reshape(top, rows).T
    table = table[jax.random.permutation(jax.random.fold_in(own, 1), rows)]
    offset_by = jax.random.randint(jax.random.fold_in(own, 2), (rows, 1), 0, top)
    return jnp.take_along_axis(table, (jnp.arange(top)[None, :] + offset_by) % top, axis=1)


def shares(count, total, bound, lean, full):
    weights = [(1 << 20) // math.isqrt(standing ** lean) + 1 for standing in range(1, count + 1)]
    largest = bound if full else min(bound, max(-(-total // count), total * weights[0] // sum(weights)))
    least = 1 if total - largest >= count - 1 else 0
    given, surplus = [largest] + [least] * (count - 1), total - largest - least * (count - 1)
    while surplus > 0:
        movable = [i for i in range(1, count) if given[i] < largest] or [i for i in range(1, count) if given[i] < bound]
        pool, left = sum([weights[i] for i in movable]), surplus
        for i in movable:
            addition = min(bound - given[i], max(1, left * weights[i] // pool), surplus)
            given[i] = given[i] + addition
            surplus = surplus - addition
    return np.array(given)


def centred(stream_key, extent, spread, most, cuts=(), held_as=jnp.bfloat16):
    drawn = jax.random.normal(stream_key, extent, jnp.float32) * spread
    if len(cuts) > 0:
        drawn = steps_of(stream_key, extent, cuts, -0.22, 0.18) * drawn
    return jnp.clip(drawn, min=-most, max=most).astype(held_as)


def setup_inputs(seed: int = 0) -> dict:
    key_of = jax.random.split(jax.random.key(seed), 9)
    point_feats = centred(key_of[0], (WIN, N_SLAB * P_DEV, C), 1.0, 6.0, ((0, 2), (1, 16)), jnp.float32)
    owner_slab_keys = jax.random.split(jax.random.fold_in(key_of[1], 1), WIN * (N_SLAB * P_DEV) // P_DEV)
    owner_slab_turns = jax.random.permutation(jax.random.fold_in(key_of[1], 3), WIN * (N_SLAB * P_DEV) // P_DEV)
    owner_slab = jax.vmap(lambda own, number: deal_out(jax.random.fold_in(key_of[1], 2), own, number, P_DEV, N_SLAB, 1, CAP, 2))(owner_slab_keys, owner_slab_turns).reshape((WIN, N_SLAB * P_DEV, 1))
    block_slot = touch_ends(jax.random.randint(key_of[2], (WIN, N_SLAB * P_DEV), 0, NB), jax.random.fold_in(key_of[2], 1), 0, NB - 1).astype(jnp.int32)
    voxel_index = touch_ends(jax.random.randint(key_of[3], (WIN, N_SLAB * P_DEV), 0, VOX), jax.random.fold_in(key_of[3], 1), 0, VOX - 1).astype(jnp.int32)
    boundary = draw_boundary(jax.random.fold_in(key_of[8], 71), 0)
    neighbours = draw_neighbours(jax.random.fold_in(key_of[8], 71), 0)
    weight_taps = centred(key_of[6], (27, C, C), (27 * C) ** -0.5, 0.109375, (), jnp.float32)
    cotangent = centred(key_of[7], (WIN, N_SLAB * NB * VOX, C), 1.0, 6.0, ((0, 2), (1, 16)), jnp.float32)
    return dict(point_feats=point_feats, owner_slab=owner_slab, block_slot=block_slot, voxel_index=voxel_index, boundary=boundary, neighbours=neighbours, weight_taps=weight_taps, cotangent=cotangent)


highest = lax.Precision.HIGHEST

def grid_tables():
    padded_edge = E + 2
    position = np.arange(padded_edge)
    section = np.where(position == 0, 0, np.where(position == padded_edge - 1, 2, 1))
    within = np.where(position == 0, E - 1, np.where(position == padded_edge - 1, 0, position - 1))
    grid_x, grid_y, grid_z = np.meshgrid(position, position, position, indexing='ij')
    tap_table = section[grid_x] * 9 + section[grid_y] * 3 + section[grid_z]
    voxel_table = within[grid_x] * E * E + within[grid_y] * E + within[grid_z]
    return (jnp.asarray(tap_table.reshape(-1), jnp.int32), jnp.asarray(voxel_table.reshape(-1), jnp.int32))

def slab_work(visible, neighbour_rows, weight_taps, grad_out):
    tap_table, voxel_table = grid_tables()
    slots_all = visible.shape[0]
    flat_visible = visible.reshape(slots_all * VOX, C)
    gather_rows = (neighbour_rows[:, tap_table] * VOX + voxel_table[None, :]).astype(jnp.int32)
    padded = flat_visible[gather_rows].reshape(NB, E + 2, E + 2, E + 2, C)
    pre_act = jnp.zeros((NB * VOX, C), jnp.float32)
    for tap_x in range(3):
        for tap_y in range(3):
            for tap_z in range(3):
                window = padded[:, tap_x:tap_x + E, tap_y:tap_y + E, tap_z:tap_z + E].reshape(NB * VOX, C)
                pre_act = pre_act + jnp.dot(window, weight_taps[tap_x * 9 + tap_y * 3 + tap_z], precision=highest, preferred_element_type=jnp.float32)
    gate_value = jax.nn.sigmoid(pre_act)
    activated = pre_act * gate_value
    grad_pre = grad_out * gate_value * (1.0 + pre_act * (1.0 - gate_value))
    grad_padded = jnp.zeros_like(padded)
    pieces = []
    for tap_x in range(3):
        for tap_y in range(3):
            for tap_z in range(3):
                window = padded[:, tap_x:tap_x + E, tap_y:tap_y + E, tap_z:tap_z + E].reshape(NB * VOX, C)
                pieces.append(jnp.dot(window.T, grad_pre, precision=highest, preferred_element_type=jnp.float32))
                back_rows = jnp.dot(grad_pre, weight_taps[tap_x * 9 + tap_y * 3 + tap_z].T, precision=highest, preferred_element_type=jnp.float32)
                grad_padded = grad_padded.at[:, tap_x:tap_x + E, tap_y:tap_y + E, tap_z:tap_z + E].add(back_rows.reshape(NB, E, E, E, C))
    weight_term = jnp.stack(pieces).reshape(27 * C, C)
    grad_visible = jnp.zeros((slots_all * VOX, C), jnp.float32).at[gather_rows.reshape(-1)].add(grad_padded.reshape(-1, C))
    return (activated, grad_visible.reshape(slots_all, VOX, C), weight_term)

def reference(point_feats, owner_slab, block_slot, voxel_index, boundary, neighbours, weight_taps, cotangent):
    row_ids = ((owner_slab[:, :, 0] * NB + block_slot) * VOX + voxel_index).astype(jnp.int32)

    def voxelize(rows_one, feats_one):
        return jnp.zeros((N_SLAB * NB * VOX, C), jnp.float32).at[rows_one].add(feats_one)
    block_feats = jax.vmap(voxelize)(row_ids, point_feats).reshape(WIN, N_SLAB, NB, VOX, C)
    before = jnp.roll(block_feats, 1, axis=1)
    after_slab = jnp.roll(block_feats, -1, axis=1)
    bound_before = jnp.roll(boundary, 1, axis=1)[:, :, 1]
    bound_after = jnp.roll(boundary, -1, axis=1)[:, :, 0]
    pick_rows = jax.vmap(jax.vmap(lambda blocks, chosen: blocks[chosen]))
    from_left = pick_rows(before, bound_before)
    from_right = pick_rows(after_slab, bound_after)
    empty_block = jnp.zeros((WIN, N_SLAB, 1, VOX, C), jnp.float32)
    visible = jnp.concatenate([block_feats, from_left, from_right, empty_block], axis=2)
    slots_all = NB + 2 * NH + 1
    visible_items = visible.reshape(WIN * N_SLAB, slots_all, VOX, C)
    neighbour_items = neighbours.reshape(WIN * N_SLAB, NB, 27)
    cotangent_items = cotangent.reshape(WIN * N_SLAB, NB * VOX, C)

    def scan_step(running, item_tuple):
        activated, grad_visible, weight_term = slab_work(item_tuple[0], item_tuple[1], weight_taps, item_tuple[2])
        return (running + weight_term, (activated, grad_visible))
    weight_sum, (activated, grad_visible) = lax.scan(scan_step, jnp.zeros((27 * C, C), jnp.float32), (visible_items, neighbour_items, cotangent_items))
    grad_visible = grad_visible.reshape(WIN, N_SLAB, slots_all, VOX, C)
    grad_own = grad_visible[:, :, :NB]
    left_grads = grad_visible[:, :, NB:NB + NH]
    right_grads = grad_visible[:, :, NB + NH:NB + 2 * NH]
    add_at = jax.vmap(jax.vmap(lambda blocks, chosen, additions: blocks.at[chosen].add(additions)))
    grad_blocks = add_at(grad_own, boundary[:, :, 0], jnp.roll(right_grads, 1, axis=1))
    grad_blocks = add_at(grad_blocks, boundary[:, :, 1], jnp.roll(left_grads, -1, axis=1))
    point_grads = jax.vmap(lambda flat_rows, row_list: flat_rows[row_list])(grad_blocks.reshape(WIN, N_SLAB * NB * VOX, C), row_ids)
    activated = activated.reshape(WIN, N_SLAB * NB * VOX, C)
    scale = 1.0 / math.sqrt(WIN * N_SLAB * NB * VOX)
    return (activated, point_grads, weight_sum * scale)
```

```python
import functools
import math

import jax
import jax.numpy as jnp
from jax import lax
from jax.experimental import pallas as pl
from jax.experimental.pallas import tpu as pltpu
from jax.sharding import PartitionSpec as P

C = 128
E = 8
NB = 2
VOX = 512
FACE = E * E
PAD = E + 2
COLS = 9 * C

f32 = jnp.float32
bf16 = jnp.bfloat16
VMEM = pl.BlockSpec(memory_space=pltpu.VMEM)
SMEM = pl.BlockSpec(memory_space=pltpu.SMEM)


def params(mib):
    return pltpu.CompilerParams(vmem_limit_bytes=mib << 20)


def struct(*shape, dtype=f32):
    return jax.ShapeDtypeStruct(shape, dtype)


def mm(a, b, dims=((1,), (0,))):
    return lax.dot_general(a, b, (dims, ((), ())), preferred_element_type=f32)


def split(value):
    high = value.astype(bf16)
    return high, (value - high.astype(f32)).astype(bf16)


def split3(value):
    high = value.astype(bf16)
    rest = value - high.astype(f32)
    middle = rest.astype(bf16)
    return high, middle, (rest - middle.astype(f32)).astype(bf16)


def iota(shape, dim):
    return lax.broadcasted_iota(jnp.int32, shape, dim)


def pack_kernel(slabs, capacity, me_ref, feats, owner, slot, vox, out, dest_out):
    points = feats.shape[0]
    block = capacity + 8
    target = owner[...]
    onehot = iota((slabs, points), 0) == target
    marks = jnp.where(onehot, 1.0, 0.0).astype(bf16)
    earlier = jnp.where(iota((points, points), 0) < iota((points, points), 1), 1.0, 0.0).astype(bf16)
    counts = mm(marks, earlier)
    rank = jnp.sum(jnp.where(onehot, counts, 0.0), axis=0, keepdims=True).astype(jnp.int32)
    place = target * block + rank
    dest_out[...] = jnp.broadcast_to(target * capacity + rank, dest_out.shape)
    chosen = jnp.where(iota((slabs * block, points), 0) == place, 1.0, 0.0).astype(bf16)
    parts = jnp.concatenate(split3(feats[...]), axis=1)
    rows = mm(chosen, parts)
    rows = rows[:, :C] + rows[:, C : 2 * C] + rows[:, 2 * C :]
    out[...] = rows.reshape(slabs, block, C)
    code = slot[...] * VOX + vox[...] + 1
    upper = lax.shift_right_logical(code, 5)
    lower = jnp.bitwise_and(code, 31)
    lane = lax.rem(me_ref[0], C // capacity) * capacity + rank
    lanes = jnp.where(iota((C, points), 0) == lane, 1.0, 0.0).astype(bf16)
    nt = ((1,), (1,))
    high = mm(jnp.where(onehot, upper, 0).astype(f32).astype(bf16), lanes, nt)
    low = mm(jnp.where(onehot, lower, 0).astype(f32).astype(bf16), lanes, nt)
    ids = high * 32.0 + low
    out[:, capacity:, :] = jnp.broadcast_to(ids[:, None, :], (slabs, 8, C))


def weights_kernel(taps, forward, backward):
    for i in range(3):
        for jk in range(9):
            tap = taps[i * 9 + jk]
            high, low = split(tap)
            rows = slice(jk * C, (jk + 1) * C)
            for part in range(2):
                forward[i, part * COLS + jk * C : part * COLS + (jk + 1) * C, :C] = high
                forward[i, part * COLS + jk * C : part * COLS + (jk + 1) * C, C:] = low
            high, low = split(tap.T)
            backward[i * C : (i + 1) * C, rows] = high
            backward[(3 + i) * C : (4 + i) * C, rows] = high
            backward[(6 + i) * C : (7 + i) * C, rows] = low


def codes_of(ids, chunk, group):
    total = ids[chunk * group]
    for t in range(1, group):
        total = total + ids[chunk * group + t]
    return total


def voxel_kernel(capacity, lent, recv, blocks, to_left, to_right, codes_out, hot):
    slabs = recv.shape[0]
    group = C // capacity
    voxels = NB * VOX
    ids = recv[:, capacity:, :]
    rows = recv[:, :capacity, :].reshape(slabs * capacity, C)
    row_parts = jnp.concatenate(split(rows), axis=1)
    numbers = iota((voxels, C), 0).astype(f32) + 1.0
    for chunk in range(slabs // group):
        codes = codes_of(ids, chunk, group)
        codes_out[chunk * 8 : (chunk + 1) * 8, :] = codes
        match = numbers == codes[:1]
        hot[:, chunk * C : (chunk + 1) * C] = jnp.where(match, 1.0, 0.0).astype(bf16)
    sums = mm(hot[...], row_parts)
    blocks[...] = sums[:, :C] + sums[:, C:]
    left = pl.multiple_of(lent[0] * VOX, VOX)
    right = pl.multiple_of(lent[1] * VOX, VOX)
    to_left[...] = blocks[pl.ds(left, FACE), :]
    to_right[...] = blocks[pl.ds(right + VOX - FACE, FACE), :]


def sublane(shape):
    return iota(shape, len(shape) - 2)


def plane_versions(first, center, last):
    three = [jnp.concatenate([first[k], center[k], last[k]], axis=0).reshape(PAD, E, C) for k in range(3)]
    z = sublane((PAD, E, C))
    down = pltpu.roll(jnp.where(z == E - 1, three[0], three[1]), 1, 1)
    up = pltpu.roll(jnp.where(z == 0, three[2], three[1]), E - 1, 1)
    return [v.reshape(PAD * E, C) for v in (down, three[1], up)]


def put_columns(columns, b, p_rows, versions):
    for k in range(3):
        for j in range(3):
            high, low = split(versions[k][E * j : E * j + FACE])
            at = (3 * j + k) * C
            columns[b, p_rows, at : at + C] = high
            columns[b, p_rows, COLS + at : COLS + at + C] = low


def load(source, block, stride, offset, size):
    return source[pl.ds(pl.multiple_of(block * stride + offset, E), size), :]


def build_plane(names, b, i, source, stride, offset, limit):
    def piece(j, k, at, size):
        name = jnp.minimum(names[b, 9 * i + 3 * j + k], limit)
        return load(source, name, stride, offset + at, size)

    first = [piece(0, k, FACE - E, E) for k in range(3)]
    center = [piece(1, k, 0, FACE) for k in range(3)]
    last = [piece(2, k, 0, E) for k in range(3)]
    return plane_versions(first, center, last)


def spread_plane(names, b, i, sums, target, stride, offset, limit):
    z = sublane((PAD, E, C))
    three = [s.reshape(PAD, E, C) for s in sums]
    down = pltpu.roll(three[0], E - 1, 1)
    up = pltpu.roll(three[2], 1, 1)
    zero = jnp.zeros_like(down)
    own = three[1] + jnp.where(z < E - 1, down, zero) + jnp.where(z > 0, up, zero)
    values = [jnp.where(z == E - 1, down, zero), own, jnp.where(z == 0, up, zero)]
    for k in range(3):
        value = values[k].reshape(PAD * E, C)
        for j, at, size, start in ((0, FACE - E, E, 0), (1, 0, FACE, E), (2, 0, E, E + FACE)):
            name = jnp.minimum(names[b, 9 * i + 3 * j + k], limit)
            where = pl.ds(pl.multiple_of(name * stride + offset + at, E), size)
            target[where, :] = target[where, :] + value[start : start + size]


def column_sums(back):
    sums = []
    for k in range(3):
        total = None
        for j in range(3):
            around = [back(3 * j + k)]
            if j > 0:
                around.insert(0, jnp.zeros((E * j, C), f32))
            if j < 2:
                around.append(jnp.zeros((E * (2 - j), C), f32))
            value = jnp.concatenate(around, axis=0)
            total = value if total is None else total + value
        sums.append(total)
    return sums


def forward_kernel(
    names, blocks, from_left, from_right, forward, backward, cotangent,
    activated, grads, columns, edge_left, edge_right,
    visible, faces_low, faces_high, edge_back, low_grads, high_grads,
):
    visible[: NB * VOX] = blocks[...]
    visible[NB * VOX :] = jnp.zeros((VOX, C), f32)
    none = jnp.zeros((FACE, C), f32)
    for b in range(NB):
        faces_low[b * FACE : (b + 1) * FACE] = blocks[(b + 1) * VOX - FACE : (b + 1) * VOX]
        faces_high[b * FACE : (b + 1) * FACE] = blocks[b * VOX : b * VOX + FACE]
    faces_low[2 * FACE : 3 * FACE] = from_left[...]
    faces_low[3 * FACE : 4 * FACE] = none
    faces_low[4 * FACE :] = none
    faces_high[2 * FACE : 3 * FACE] = none
    faces_high[3 * FACE : 4 * FACE] = from_right[...]
    faces_high[4 * FACE :] = none
    low_grads[...] = jnp.zeros_like(low_grads)
    high_grads[...] = jnp.zeros_like(high_grads)
    grads[...] = jnp.zeros_like(grads)
    for b in range(NB):
        put_columns(columns, b, slice(0, FACE), build_plane(names, b, 0, faces_low, FACE, 0, 4))
        put_columns(
            columns, b, slice((PAD - 1) * FACE, PAD * FACE), build_plane(names, b, 2, faces_high, FACE, 0, 4)
        )

        @pl.loop(1, E + 1)
        def _(p):
            planes = build_plane(names, b, 1, visible, VOX, (p - 1) * FACE, 2)
            put_columns(columns, b, pl.ds(pl.multiple_of(p * FACE, FACE), FACE), planes)

        total = None
        for i in range(3):
            term = mm(columns[b, FACE * i : FACE * i + VOX, :], forward[i])
            total = term if total is None else total + term
        pre = total[:, :C] + total[:, C:]
        here = slice(b * VOX, (b + 1) * VOX)
        gate = jax.nn.sigmoid(pre)
        activated[here] = pre * gate
        grad = cotangent[here] * gate * (1.0 + pre * (1.0 - gate))
        high, low = split(grad)
        for i in range(3):
            at = slice(FACE * i, FACE * i + VOX)
            grads[b, at, i * C : (i + 1) * C] = high
            grads[b, at, (3 + i) * C : (4 + i) * C] = low
            grads[b, at, (6 + i) * C : (7 + i) * C] = high
    for i, p, target in ((0, 0, low_grads), (2, PAD - 1, high_grads)):
        here = slice(p * FACE, (p + 1) * FACE)
        for b in range(NB):
            edge_back[b * FACE : (b + 1) * FACE] = sum(
                mm(grads[b, here, part * C : (part + 1) * C], backward[part * C : (part + 1) * C, :])
                for part in (i, 3 + i, 6 + i)
            )
        for b in range(NB):
            sums = column_sums(lambda jk: edge_back[b * FACE : (b + 1) * FACE, jk * C : (jk + 1) * C])
            spread_plane(names, b, i, sums, target, FACE, 0, 4)
    edge_left[...] = low_grads[2 * FACE : 3 * FACE]
    edge_right[...] = high_grads[3 * FACE : 4 * FACE]


def weight_grad_kernel(places, columns, grads, out, total):
    for i in range(3):
        for b in range(NB):
            here = slice(FACE * i, FACE * i + VOX)
            pair = jnp.concatenate(
                [grads[b, here, i * C : (i + 1) * C], grads[b, here, (3 + i) * C : (4 + i) * C]], axis=1
            )
            term = mm(columns[b, here, :], pair, ((0,), (0,)))
            total[...] = term if b == 0 else total[...] + term
        value = total[:COLS, :C] + total[:COLS, C:] + total[COLS:, :C] + total[COLS:, C:]
        for start, stop, to in places:
            low, high = max(start, i * COLS), min(stop, (i + 1) * COLS)
            if low < high:
                out[to + low - start : to + high - start] = value[low - i * COLS : high - i * COLS]


def backward_kernel(names, lent, grads, backward, halo_left, halo_right, blocks_out, back, target):
    target[...] = jnp.zeros_like(target)
    for b in range(NB):
        back[...] = mm(grads[b], backward[...])

        def plane(i, p, offset):
            rows = pl.ds(pl.multiple_of(p * FACE, FACE), FACE)
            sums = column_sums(lambda jk: back[rows, jk * C : (jk + 1) * C])
            spread_plane(names, b, i, sums, target, VOX, offset, 2)

        plane(0, 0, VOX - FACE)
        plane(2, PAD - 1, 0)

        @pl.loop(1, E + 1)
        def _(p):
            plane(1, p, (p - 1) * FACE)

    left = pl.multiple_of(lent[0] * VOX, VOX)
    right = pl.multiple_of(lent[1] * VOX, VOX) + VOX - FACE
    target[pl.ds(left, FACE), :] = target[pl.ds(left, FACE), :] + halo_left[...]
    target[pl.ds(right, FACE), :] = target[pl.ds(right, FACE), :] + halo_right[...]
    blocks_out[...] = target[: NB * VOX]


def gather_kernel(grad_blocks, codes, out):
    parts = jnp.concatenate(split(grad_blocks[...]), axis=1)
    voxels = NB * VOX
    by_row = codes[...].T
    numbers = iota((C, voxels), 1).astype(f32) + 1.0
    for chunk in range(codes.shape[0] // 8):
        match = numbers == by_row[:, chunk * 8 : chunk * 8 + 1]
        rows = mm(jnp.where(match, 1.0, 0.0).astype(bf16), parts)
        out[chunk * C : (chunk + 1) * C] = rows[:, :C] + rows[:, C:]


def unpack_kernel(came_back, dest, out):
    places = dest[...].astype(f32).T[:, :1]
    points, slots = out.shape[0], came_back.shape[0]
    chosen = jnp.where(iota((points, slots), 1).astype(f32) == places, 1.0, 0.0).astype(bf16)
    rows = mm(chosen, jnp.concatenate(split3(came_back[...]), axis=1))
    out[...] = rows[:, :C] + rows[:, C : 2 * C] + rows[:, 2 * C :]


def bit_reversed(number, bits):
    return int(format(number, f"0{bits}b")[::-1], 2)


def per_device(
    point_feats, owner_slab, block_slot, voxel_index, boundary, neighbours, weight_taps, cotangent
):
    slabs = lax.axis_size("slab")
    windows = lax.axis_size("dp")
    points = point_feats.shape[1]
    capacity = 2 * points // slabs
    bits = slabs.bit_length() - 1
    me = lax.axis_index("slab")
    names = neighbours[0]
    lent = boundary.reshape(2)
    voxels = NB * VOX
    chunk = 27 * C // slabs

    send, dest = pl.pallas_call(
        functools.partial(pack_kernel, slabs, capacity),
        out_shape=(struct(slabs, capacity + 8, C), struct(8, points, dtype=jnp.int32)),
        in_specs=[SMEM] + [VMEM] * 4,
        out_specs=(VMEM, VMEM),
        compiler_params=params(32),
        name="pack",
    )(me.reshape(1), point_feats[0], owner_slab.reshape(1, points), block_slot, voxel_index)
    recv = lax.all_to_all(send, "slab", split_axis=0, concat_axis=0, tiled=True)
    forward, backward = pl.pallas_call(
        weights_kernel,
        out_shape=(struct(3, 2 * COLS, 2 * C, dtype=bf16), struct(9 * C, COLS, dtype=bf16)),
        in_specs=[VMEM],
        out_specs=(VMEM, VMEM),
        compiler_params=params(32),
        name="weights",
    )(weight_taps)
    blocks, to_left, to_right, codes = pl.pallas_call(
        functools.partial(voxel_kernel, capacity),
        out_shape=(
            struct(voxels, C), struct(FACE, C), struct(FACE, C), struct(slabs * capacity // C * 8, C)
        ),
        in_specs=[SMEM, VMEM],
        out_specs=(VMEM,) * 4,
        scratch_shapes=[pltpu.VMEM((voxels, slabs * capacity), bf16)],
        compiler_params=params(32),
        name="voxels",
    )(lent, recv)
    up = [(i, (i + 1) % slabs) for i in range(slabs)]
    down = [(j, i) for i, j in up]
    from_left = lax.ppermute(to_right, "slab", up)
    from_right = lax.ppermute(to_left, "slab", down)
    activated, grads, columns, edge_left, edge_right = pl.pallas_call(
        forward_kernel,
        out_shape=(
            struct(voxels, C),
            struct(NB, PAD * FACE, 9 * C, dtype=bf16),
            struct(NB, PAD * FACE, 2 * COLS, dtype=bf16),
            struct(FACE, C),
            struct(FACE, C),
        ),
        in_specs=[SMEM] + [VMEM] * 6,
        out_specs=(VMEM,) * 5,
        scratch_shapes=[
            pltpu.VMEM((3 * VOX, C), f32),
            pltpu.VMEM((5 * FACE, C), f32),
            pltpu.VMEM((5 * FACE, C), f32),
            pltpu.VMEM((NB * FACE, COLS), f32),
            pltpu.VMEM((5 * FACE, C), f32),
            pltpu.VMEM((5 * FACE, C), f32),
        ],
        compiler_params=params(40),
        name="forward",
    )(names, blocks, from_left, from_right, forward, backward, cotangent[0])
    halo_right = lax.ppermute(edge_left, "slab", down)
    halo_left = lax.ppermute(edge_right, "slab", up)

    aligned = chunk % 8 == 0
    places = tuple(
        (c * chunk, (c + 1) * chunk, (bit_reversed(c, bits) if aligned else c) * chunk) for c in range(slabs)
    )
    if not aligned:
        places = ((0, 27 * C, 0),)
    term = pl.pallas_call(
        functools.partial(weight_grad_kernel, places),
        out_shape=struct(27 * C, C),
        in_specs=[VMEM, VMEM],
        out_specs=VMEM,
        scratch_shapes=[pltpu.VMEM((2 * COLS, 2 * C), f32)],
        compiler_params=params(40),
        name="weight_grad",
    )(columns, grads)
    if not aligned:
        order = [bit_reversed(c, bits) for c in range(slabs)]
        term = term.reshape(slabs, chunk, C)[jnp.array(order)].reshape(27 * C, C)
    grad_blocks = pl.pallas_call(
        backward_kernel,
        out_shape=struct(voxels, C),
        in_specs=[SMEM, SMEM] + [VMEM] * 4,
        out_specs=VMEM,
        scratch_shapes=[pltpu.VMEM((PAD * FACE, COLS), f32), pltpu.VMEM((3 * VOX, C), f32)],
        compiler_params=params(40),
        name="backward",
    )(names, lent, grads, backward, halo_left, halo_right)
    back_points = pl.pallas_call(
        gather_kernel,
        out_shape=struct(slabs * capacity, C),
        in_specs=[VMEM, VMEM],
        out_specs=VMEM,
        compiler_params=params(32),
        name="gather",
    )(grad_blocks, codes)
    came_back = lax.all_to_all(
        back_points.reshape(slabs, capacity, C), "slab", split_axis=0, concat_axis=0, tiled=True
    )
    point_grads = pl.pallas_call(
        unpack_kernel,
        out_shape=struct(points, C),
        in_specs=[VMEM, VMEM],
        out_specs=VMEM,
        compiler_params=params(32),
        name="unpack",
    )(came_back.reshape(slabs * capacity, C), dest)

    share = term
    for bit in range(bits):
        side = lax.shift_right_logical(me, bit) & 1
        half = share.shape[0] // 2
        kept = lax.dynamic_slice_in_dim(share, side * half, half, 0)
        sent = lax.dynamic_slice_in_dim(share, (1 - side) * half, half, 0)
        share = kept + lax.ppermute(sent, "slab", [(i, i ^ (1 << bit)) for i in range(slabs)])
    step = 1
    while step < windows:
        share = share + lax.ppermute(share, "dp", [(i, i ^ step) for i in range(windows)])
        step *= 2
    scale = 1.0 / math.sqrt(windows * slabs * voxels)
    return (activated[None], point_grads[None], share * scale)


def solution(mesh):
    return jax.shard_map(
        per_device,
        mesh=mesh,
        in_specs=(
            P("dp", "slab", None),
            P("dp", "slab", None),
            P("dp", "slab"),
            P("dp", "slab"),
            P("dp", "slab", None, None),
            P("dp", "slab", None),
            P(),
            P("dp", "slab", None),
        ),
        out_specs=(P("dp", "slab", None), P("dp", "slab", None), P("slab", None)),
        check_vma=False,
    )
```

```python
import functools
import math

import jax
import jax.numpy as jnp
from jax import lax
from jax.experimental import pallas as pl
from jax.experimental.pallas import tpu as pltpu
from jax.sharding import PartitionSpec as P

C = 128
E = 8
NB = 2
VOX = 512
FACE = E * E
PAD = E + 2
COLS = 9 * C

f32 = jnp.float32
bf16 = jnp.bfloat16
VMEM = pl.BlockSpec(memory_space=pltpu.VMEM)
SMEM = pl.BlockSpec(memory_space=pltpu.SMEM)
ANY = pl.BlockSpec(memory_space=pl.ANY)
HBM = pl.BlockSpec(memory_space=pltpu.HBM)


def params(mib):
    return pltpu.CompilerParams(vmem_limit_bytes=mib << 20)


def cost(microseconds):
    return pl.CostEstimate(flops=int(microseconds * 1e9), bytes_accessed=0, transcendentals=0)


def struct(*shape, dtype=f32):
    return jax.ShapeDtypeStruct(shape, dtype)


def mm(a, b, dims=((1,), (0,))):
    return lax.dot_general(a, b, (dims, ((), ())), preferred_element_type=f32)


def split(value):
    high = value.astype(bf16)
    return high, (value - high.astype(f32)).astype(bf16)


def split3(value):
    high = value.astype(bf16)
    rest = value - high.astype(f32)
    middle = rest.astype(bf16)
    return high, middle, (rest - middle.astype(f32)).astype(bf16)


def iota(shape, dim):
    return lax.broadcasted_iota(jnp.int32, shape, dim)


def pack_kernel(
    slabs, capacity, me_ref, feats_in, owner_in, slot_in, vox_in, out, dest_out, feats, owner, slot, vox, sems
):
    copies = [
        pltpu.make_async_copy(source, target, sems.at[n])
        for n, (source, target) in enumerate(
            ((owner_in, owner), (slot_in, slot), (vox_in, vox), (feats_in, feats))
        )
    ]
    for copy in copies:
        copy.start()
    points = feats.shape[0]
    block = capacity + 8
    for copy in copies[:3]:
        copy.wait()
    target = owner[...]
    onehot = iota((slabs, points), 0) == target
    marks = jnp.where(onehot, 1.0, 0.0).astype(bf16)
    earlier = jnp.where(iota((points, points), 0) < iota((points, points), 1), 1.0, 0.0).astype(bf16)
    counts = mm(marks, earlier)
    rank = jnp.sum(jnp.where(onehot, counts, 0.0), axis=0, keepdims=True).astype(jnp.int32)
    place = target * block + rank
    dest_out[...] = jnp.broadcast_to(target * capacity + rank, dest_out.shape)
    chosen = jnp.where(iota((slabs * block, points), 0) == place, 1.0, 0.0).astype(bf16)
    copies[3].wait()
    parts = jnp.concatenate(split3(feats[...]), axis=1)
    rows = mm(chosen, parts)
    rows = rows[:, :C] + rows[:, C : 2 * C] + rows[:, 2 * C :]
    out[...] = rows.reshape(slabs, block, C)
    code = slot[...] * VOX + vox[...] + 1
    upper = lax.shift_right_logical(code, 5)
    lower = jnp.bitwise_and(code, 31)
    lane = lax.rem(me_ref[0], C // capacity) * capacity + rank
    lanes = jnp.where(iota((C, points), 0) == lane, 1.0, 0.0).astype(bf16)
    nt = ((1,), (1,))
    high = mm(jnp.where(onehot, upper, 0).astype(f32).astype(bf16), lanes, nt)
    low = mm(jnp.where(onehot, lower, 0).astype(f32).astype(bf16), lanes, nt)
    ids = high * 32.0 + low
    out[:, capacity:, :] = jnp.broadcast_to(ids[:, None, :], (slabs, 8, C))


def weights_kernel(taps, backward):
    for i in range(3):
        for jk in range(9):
            high, low = split(taps[i * 9 + jk].T)
            columns = slice(jk * C, (jk + 1) * C)
            backward[i * C : (i + 1) * C, columns] = high
            backward[(3 + i) * C : (4 + i) * C, columns] = high
            backward[(6 + i) * C : (7 + i) * C, columns] = low


def split_taps(taps, forward):
    for i in range(3):
        for jk in range(9):
            high, low = split(taps[i * 9 + jk])
            for part in range(2):
                rows = slice(part * COLS + jk * C, part * COLS + (jk + 1) * C)
                forward[i, rows, :C] = high
                forward[i, rows, C:] = low


def codes_of(ids, chunk, group):
    total = ids[chunk * group]
    for t in range(1, group):
        total = total + ids[chunk * group + t]
    return total


def received(recv, capacity):
    slabs = recv.shape[0]
    rows = recv[:, :capacity, :].reshape(slabs * capacity, C)
    return recv[:, capacity:, :], jnp.concatenate(split(rows), axis=1)


def faces_kernel(capacity, lent, me, recv, to_core, to_far):
    group = C // capacity
    ids, row_parts = received(recv, capacity)
    row = iota((2 * FACE, C), 0)
    number = jnp.where(row < FACE, lent[0] * VOX + row, lent[1] * VOX + VOX - 2 * FACE + row)
    number = number.astype(f32) + 1.0
    hot = []
    for chunk in range(recv.shape[0] // group):
        match = number == codes_of(ids, chunk, group)[:1]
        hot.append(jnp.where(match, 1.0, 0.0).astype(bf16))
    sums = mm(jnp.concatenate(hot, axis=1), row_parts)
    sums = sums[:, :C] + sums[:, C:]
    even = jnp.bitwise_and(me[0], 1) == 0
    to_core[...] = jnp.where(even, sums[FACE:], sums[:FACE])
    to_far[...] = jnp.where(even, sums[:FACE], sums[FACE:])


def sublane(shape):
    return iota(shape, len(shape) - 2)


def plane_versions(first, center, last):
    three = [jnp.concatenate([first[k], center[k], last[k]], axis=0).reshape(PAD, E, C) for k in range(3)]
    z = sublane((PAD, E, C))
    down = pltpu.roll(jnp.where(z == E - 1, three[0], three[1]), 1, 1)
    up = pltpu.roll(jnp.where(z == 0, three[2], three[1]), E - 1, 1)
    return [v.reshape(PAD * E, C) for v in (down, three[1], up)]


def put_columns(columns, at_first, rows, versions):
    for k in range(3):
        for j in range(3):
            high, low = split(versions[k][E * j : E * j + FACE])
            at = (3 * j + k) * C
            columns[at_first, rows, at : at + C] = high
            columns[at_first, rows, COLS + at : COLS + at + C] = low


def load(source, block, stride, offset, size):
    return source[pl.ds(pl.multiple_of(block * stride + offset, E), size), :]


def build_plane(names, b, i, source, stride, offset, limit):
    def piece(j, k, at, size):
        name = jnp.minimum(names[b, 9 * i + 3 * j + k], limit)
        return load(source, name, stride, offset + at, size)

    first = [piece(0, k, FACE - E, E) for k in range(3)]
    center = [piece(1, k, 0, FACE) for k in range(3)]
    last = [piece(2, k, 0, E) for k in range(3)]
    return plane_versions(first, center, last)


def spread_plane(names, b, i, sums, target, stride, offset, limit):
    z = sublane((PAD, E, C))
    three = [s.reshape(PAD, E, C) for s in sums]
    down = pltpu.roll(three[0], E - 1, 1)
    up = pltpu.roll(three[2], 1, 1)
    zero = jnp.zeros_like(down)
    own = three[1] + jnp.where(z < E - 1, down, zero) + jnp.where(z > 0, up, zero)
    values = [jnp.where(z == E - 1, down, zero), own, jnp.where(z == 0, up, zero)]
    for k in range(3):
        value = values[k].reshape(PAD * E, C)
        for j, at, size, start in ((0, FACE - E, E, 0), (1, 0, FACE, E), (2, 0, E, E + FACE)):
            name = jnp.minimum(names[b, 9 * i + 3 * j + k], limit)
            where = pl.ds(pl.multiple_of(name * stride + offset + at, E), size)
            target[where, :] = target[where, :] + value[start : start + size]


def column_sums(back):
    sums = []
    for k in range(3):
        total = None
        for j in range(3):
            around = [back(3 * j + k)]
            if j > 0:
                around.insert(0, jnp.zeros((E * j, C), f32))
            if j < 2:
                around.append(jnp.zeros((E * (2 - j), C), f32))
            value = jnp.concatenate(around, axis=0)
            total = value if total is None else total + value
        sums.append(total)
    return sums


def interior_kernel(
    capacity, names_in, recv, taps_in,
    before, columns, faces, codes_out, forward,
    names, visible, hot, taps, sems,
):
    names_copy = pltpu.make_async_copy(names_in, names, sems.at[0])
    taps_copy = pltpu.make_async_copy(taps_in, taps, sems.at[1])
    names_copy.start()
    taps_copy.start()
    voxels = NB * VOX
    group = C // capacity
    ids, row_parts = received(recv, capacity)
    numbers = iota((voxels, C), 0).astype(f32) + 1.0
    for chunk in range(recv.shape[0] // group):
        codes = codes_of(ids, chunk, group)
        codes_out[chunk * 8 : (chunk + 1) * 8, :] = codes
        match = numbers == codes[:1]
        hot[:, chunk * C : (chunk + 1) * C] = jnp.where(match, 1.0, 0.0).astype(bf16)
    sums = mm(hot[...], row_parts)
    visible[:voxels] = sums[:, :C] + sums[:, C:]
    visible[voxels:] = jnp.zeros((VOX, C), f32)
    for b in range(NB):
        faces[b * FACE : (b + 1) * FACE] = visible[(b + 1) * VOX - FACE : (b + 1) * VOX]
        faces[(NB + b) * FACE : (NB + b + 1) * FACE] = visible[b * VOX : b * VOX + FACE]
    names_copy.wait()
    for b in range(NB):

        @pl.loop(1, E + 1)
        def _(p):
            planes = build_plane(names, b, 1, visible, VOX, (p - 1) * FACE, 2)
            put_columns(columns, b, pl.ds(pl.multiple_of((p - 1) * FACE, FACE), FACE), planes)

    taps_copy.wait()
    split_taps(taps, forward)
    for b in range(NB):
        start = b * VOX
        total = mm(columns[b], forward[1])
        before[start : start + VOX] = total[:, :C] + total[:, C:]
        total = mm(columns[b, : VOX - FACE, :], forward[0])
        here = slice(start + FACE, start + VOX)
        before[here] = before[here] + total[:, :C] + total[:, C:]
        total = mm(columns[b, FACE:, :], forward[2])
        here = slice(start, start + VOX - FACE)
        before[here] = before[here] + total[:, :C] + total[:, C:]


def finish_kernel(
    names_in, me, before, faces, from_core, from_far, forward, backward_in, cotangent_in,
    activated, grads, outer, to_core, to_far,
    names, faces_low, faces_high, pre, cotangent, backward, edge_back, low_grads, high_grads, sems,
):
    copies = [
        pltpu.make_async_copy(names_in, names, sems.at[0]),
        pltpu.make_async_copy(cotangent_in, cotangent, sems.at[1]),
    ]
    for n, i in enumerate((0, 2)):
        for part in (0, 3, 6):
            rows = pl.ds((i + part) * C, C)
            copies.append(
                pltpu.make_async_copy(
                    backward_in.at[rows], backward.at[pl.ds((3 * n + part // 3) * C, C)], sems.at[len(copies)]
                )
            )
    for copy in copies:
        copy.start()
    even = jnp.bitwise_and(me[0], 1) == 0
    none = jnp.zeros((FACE, C), f32)
    faces_low[: 2 * FACE] = faces[: 2 * FACE]
    faces_low[2 * FACE : 3 * FACE] = jnp.where(even, from_far[...], from_core[...])
    faces_low[3 * FACE : 4 * FACE] = none
    faces_low[4 * FACE :] = none
    faces_high[: 2 * FACE] = faces[2 * FACE :]
    faces_high[2 * FACE : 3 * FACE] = none
    faces_high[3 * FACE : 4 * FACE] = jnp.where(even, from_core[...], from_far[...])
    faces_high[4 * FACE :] = none
    low_grads[...] = jnp.zeros_like(low_grads)
    high_grads[...] = jnp.zeros_like(high_grads)
    pre[...] = before[...]
    copies[0].wait()
    for n, (i, x, source) in enumerate(((0, 0, faces_low), (2, E - 1, faces_high))):
        for b in range(NB):
            rows = slice(b * FACE, (b + 1) * FACE)
            put_columns(outer, n, rows, build_plane(names, b, i, source, FACE, 0, 4))
        total = mm(outer[n], forward[i])
        total = total[:, :C] + total[:, C:]
        for b in range(NB):
            here = slice(b * VOX + x * FACE, b * VOX + (x + 1) * FACE)
            pre[here] = pre[here] + total[b * FACE : (b + 1) * FACE]
    value = pre[...]
    gate = jax.nn.sigmoid(value)
    activated[...] = value * gate
    copies[1].wait()
    high, low = split(cotangent[...] * gate * (1.0 + value * (1.0 - gate)))
    grads[:, :C] = high
    grads[:, C:] = low
    for copy in copies[2:]:
        copy.wait()
    for n, (i, x, target) in enumerate(((0, 0, low_grads), (2, E - 1, high_grads))):
        both = jnp.concatenate([grads[b * VOX + x * FACE : b * VOX + (x + 1) * FACE, :] for b in range(NB)], axis=0)
        three = jnp.concatenate([both, both[:, :C]], axis=1)
        edge_back[...] = mm(three, backward[3 * n * C : 3 * (n + 1) * C, :])
        for b in range(NB):
            sums = column_sums(lambda jk: edge_back[b * FACE : (b + 1) * FACE, jk * C : (jk + 1) * C])
            spread_plane(names, b, i, sums, target, FACE, 0, 4)
    left = low_grads[2 * FACE : 3 * FACE]
    right = high_grads[3 * FACE : 4 * FACE]
    to_core[...] = jnp.where(even, right, left)
    to_far[...] = jnp.where(even, left, right)


def weight_grad_kernel(chunk, starts, me, columns, outer, grads, kept, sent, total, ordered):
    tn = ((0,), (0,))
    for i in range(3):
        low, high = max(i - 1, 0), E + min(i - 1, 0)
        for b in range(NB):
            x = b * E + 1 - i
            term = mm(columns[b, low * FACE : high * FACE, :], grads[(x + low) * FACE : (x + high) * FACE, :], tn)
            total[...] = term if b == 0 else total[...] + term
        if i != 1:
            x = 0 if i == 0 else E - 1
            faces = [grads[(b * E + x) * FACE : (b * E + x + 1) * FACE, :] for b in range(NB)]
            total[...] = total[...] + mm(outer[i // 2], jnp.concatenate(faces, axis=0), tn)
        value = total[:COLS, :C] + total[:COLS, C:] + total[COLS:, :C] + total[COLS:, C:]
        ordered[i * COLS : (i + 1) * COLS] = value
    first = jnp.bitwise_and(me[0], 1) == 0
    for n, to in enumerate(starts):
        even = ordered[2 * n * chunk : (2 * n + 1) * chunk]
        odd = ordered[(2 * n + 1) * chunk : (2 * n + 2) * chunk]
        kept[to : to + chunk] = jnp.where(first, even, odd)
        sent[to : to + chunk] = jnp.where(first, odd, even)


def halve(kept, arrived, side):
    half = kept.shape[0] // 2

    def part(which):
        return lax.dynamic_slice_in_dim(kept, which * half, half, 0) + lax.dynamic_slice_in_dim(
            arrived, which * half, half, 0
        )

    return part(side), part(1 - side)


def backward_kernel(names_in, grads, backward_in, blocks_out, names, backward, shifted, back, target, sems):
    copies = [
        pltpu.make_async_copy(names_in, names, sems.at[0]),
        pltpu.make_async_copy(backward_in, backward, sems.at[1]),
    ]
    for copy in copies:
        copy.start()
    target[...] = jnp.zeros_like(target)
    shifted[...] = jnp.zeros_like(shifted)
    copies[0].wait()
    for b in range(NB):
        rows = slice(b * VOX, (b + 1) * VOX)
        for i in range(3):
            at = slice(FACE * i, FACE * i + VOX)
            shifted[at, i * C : (i + 1) * C] = grads[rows, :C]
            shifted[at, (3 + i) * C : (4 + i) * C] = grads[rows, C:]
            shifted[at, (6 + i) * C : (7 + i) * C] = grads[rows, :C]
        if b == 0:
            copies[1].wait()
        back[...] = mm(shifted[...], backward[...])

        def plane(i, p, offset):
            rows = pl.ds(pl.multiple_of(p * FACE, FACE), FACE)
            sums = column_sums(lambda jk: back[rows, jk * C : (jk + 1) * C])
            spread_plane(names, b, i, sums, target, VOX, offset, 2)

        plane(0, 0, VOX - FACE)
        plane(2, PAD - 1, 0)

        @pl.loop(1, E + 1)
        def _(p):
            plane(1, p, (p - 1) * FACE)

    blocks_out[...] = target[: NB * VOX]


def gather_kernel(lent, me, grad_blocks, halo_core, halo_far, codes, out, target):
    voxels = NB * VOX
    even = jnp.bitwise_and(me[0], 1) == 0
    target[...] = grad_blocks[...]
    left = pl.ds(pl.multiple_of(lent[0] * VOX, VOX), FACE)
    right = pl.ds(pl.multiple_of(lent[1] * VOX, VOX) + VOX - FACE, FACE)
    target[left, :] = target[left, :] + jnp.where(even, halo_far[...], halo_core[...])
    target[right, :] = target[right, :] + jnp.where(even, halo_core[...], halo_far[...])
    parts = jnp.concatenate(split(target[...]), axis=1)
    by_row = codes[...].T
    numbers = iota((C, voxels), 1).astype(f32) + 1.0
    for chunk in range(codes.shape[0] // 8):
        match = numbers == by_row[:, chunk * 8 : chunk * 8 + 1]
        rows = mm(jnp.where(match, 1.0, 0.0).astype(bf16), parts)
        out[chunk * C : (chunk + 1) * C] = rows[:, :C] + rows[:, C:]


def unpack_kernel(came_back, dest, out):
    places = dest[...].astype(f32).T[:, :1]
    points, slots = out.shape[0], came_back.shape[0]
    chosen = jnp.where(iota((points, slots), 1).astype(f32) == places, 1.0, 0.0).astype(bf16)
    rows = mm(chosen, jnp.concatenate(split3(came_back[...]), axis=1))
    out[...] = rows[:, :C] + rows[:, C : 2 * C] + rows[:, 2 * C :]


def bit_reversed(number, bits):
    return int(format(number, f"0{bits}b")[::-1], 2)


def per_device(
    point_feats, owner_slab, block_slot, voxel_index, boundary, neighbours, weight_taps, cotangent
):
    slabs = lax.axis_size("slab")
    windows = lax.axis_size("dp")
    points = point_feats.shape[1]
    capacity = 2 * points // slabs
    bits = slabs.bit_length() - 1
    me = lax.axis_index("slab")
    names = neighbours[0]
    lent = boundary.reshape(2)
    voxels = NB * VOX
    chunk = 27 * C // slabs

    send, dest = pl.pallas_call(
        functools.partial(pack_kernel, slabs, capacity),
        out_shape=(struct(slabs, capacity + 8, C), struct(8, points, dtype=jnp.int32)),
        in_specs=[SMEM] + [HBM] * 4,
        out_specs=(VMEM, VMEM),
        scratch_shapes=[pltpu.VMEM((points, C), f32)]
        + [pltpu.VMEM((1, points), jnp.int32)] * 3
        + [pltpu.SemaphoreType.DMA((4,))],
        compiler_params=params(60),
        name="pack",
        cost_estimate=cost(2),
    )(me.reshape(1), point_feats[0], owner_slab.reshape(1, points), block_slot, voxel_index)
    send, weight_taps = lax.optimization_barrier((send, weight_taps))
    recv = lax.all_to_all(send, "slab", split_axis=0, concat_axis=0, tiled=True)
    backward = pl.pallas_call(
        weights_kernel,
        out_shape=struct(9 * C, COLS, dtype=bf16),
        in_specs=[VMEM],
        out_specs=VMEM,
        compiler_params=params(4),
        name="weights",
        cost_estimate=cost(0.6),
    )(weight_taps)
    recv, backward = lax.optimization_barrier((recv, backward))
    to_core, to_far = pl.pallas_call(
        functools.partial(faces_kernel, capacity),
        out_shape=(struct(FACE, C), struct(FACE, C)),
        in_specs=[SMEM, SMEM, VMEM],
        out_specs=(VMEM,) * 2,
        compiler_params=params(8),
        name="faces",
        cost_estimate=cost(0.8),
    )(lent, me.reshape(1), recv)
    core_pairs = [(i, i ^ 1) for i in range(slabs)]
    far_pairs = [(i, (i - 1 if i % 2 == 0 else i + 1) % slabs) for i in range(slabs)]
    from_core = lax.ppermute(to_core, "slab", core_pairs)
    from_far = lax.ppermute(to_far, "slab", far_pairs)
    before, columns, faces, codes, forward = pl.pallas_call(
        functools.partial(interior_kernel, capacity),
        out_shape=(
            struct(voxels, C),
            struct(NB, VOX, 2 * COLS, dtype=bf16),
            struct(2 * NB * FACE, C),
            struct(slabs * capacity // C * 8, C),
            struct(3, 2 * COLS, 2 * C, dtype=bf16),
        ),
        in_specs=[ANY, VMEM, ANY],
        out_specs=(VMEM,) * 5,
        scratch_shapes=[
            pltpu.SMEM((NB, 27), jnp.int32),
            pltpu.VMEM((3 * VOX, C), f32),
            pltpu.VMEM((voxels, slabs * capacity), bf16),
            pltpu.VMEM(weight_taps.shape, f32),
            pltpu.SemaphoreType.DMA((2,)),
        ],
        compiler_params=params(16),
        name="interior",
        cost_estimate=cost(6.5),
    )(names, recv, weight_taps)
    activated, grads, outer, edge_core, edge_far = pl.pallas_call(
        finish_kernel,
        out_shape=(
            struct(voxels, C),
            struct(voxels, 2 * C, dtype=bf16),
            struct(2, NB * FACE, 2 * COLS, dtype=bf16),
            struct(FACE, C),
            struct(FACE, C),
        ),
        in_specs=[ANY, SMEM] + [VMEM] * 5 + [ANY] * 2,
        out_specs=(VMEM,) * 5,
        scratch_shapes=[
            pltpu.SMEM((NB, 27), jnp.int32),
            pltpu.VMEM((5 * FACE, C), f32),
            pltpu.VMEM((5 * FACE, C), f32),
            pltpu.VMEM((voxels, C), f32),
            pltpu.VMEM((voxels, C), f32),
            pltpu.VMEM((6 * C, COLS), bf16),
            pltpu.VMEM((NB * FACE, COLS), f32),
            pltpu.VMEM((5 * FACE, C), f32),
            pltpu.VMEM((5 * FACE, C), f32),
            pltpu.SemaphoreType.DMA((8,)),
        ],
        compiler_params=params(14),
        name="finish",
        cost_estimate=cost(2.8),
    )(names, me.reshape(1), before, faces, from_core, from_far, forward, backward, cotangent[0])
    starts = tuple(bit_reversed(n, bits - 1) * chunk for n in range(slabs // 2))
    kept, sent = pl.pallas_call(
        functools.partial(weight_grad_kernel, chunk, starts),
        out_shape=(struct(27 * C // 2, C),) * 2,
        in_specs=[SMEM] + [VMEM] * 3,
        out_specs=(VMEM, VMEM),
        scratch_shapes=[pltpu.VMEM((2 * COLS, 2 * C), f32), pltpu.VMEM((27 * C, C), f32)],
        compiler_params=params(14),
        name="weight_grad",
        cost_estimate=cost(4),
    )(me.reshape(1), columns, outer, grads)
    def swapped(part, axis, bit):
        size = lax.axis_size(axis)
        return lax.ppermute(part, axis, [(i, i ^ (1 << bit)) for i in range(size)])

    def side(bit):
        return lax.shift_right_logical(me, bit) & 1

    halo_far = lax.ppermute(edge_far, "slab", far_pairs)
    halo_core = lax.ppermute(edge_core, "slab", core_pairs)
    sent, halo_far, halo_core = lax.optimization_barrier((sent, halo_far, halo_core))
    kept, sent = halve(kept, swapped(sent, "slab", 0), side(1))
    sent, grads = lax.optimization_barrier((sent, grads))
    arrived = swapped(sent, "slab", 1)
    grad_blocks = pl.pallas_call(
        backward_kernel,
        out_shape=struct(voxels, C),
        in_specs=[ANY, VMEM, ANY],
        out_specs=VMEM,
        scratch_shapes=[
            pltpu.SMEM((NB, 27), jnp.int32),
            pltpu.VMEM((9 * C, COLS), bf16),
            pltpu.VMEM((PAD * FACE, 9 * C), bf16),
            pltpu.VMEM((PAD * FACE, COLS), f32),
            pltpu.VMEM((3 * VOX, C), f32),
            pltpu.SemaphoreType.DMA((2,)),
        ],
        compiler_params=params(14),
        name="backward",
        cost_estimate=cost(6.5),
    )(names, grads, backward)
    arrived, grad_blocks = lax.optimization_barrier((arrived, grad_blocks))
    kept, sent = halve(kept, arrived, side(2))
    sent, grad_blocks = lax.optimization_barrier((sent, grad_blocks))
    arrived = swapped(sent, "slab", 2)
    back_points = pl.pallas_call(
        gather_kernel,
        out_shape=struct(slabs * capacity, C),
        in_specs=[SMEM] * 2 + [VMEM] * 4,
        out_specs=VMEM,
        scratch_shapes=[pltpu.VMEM((voxels, C), f32)],
        compiler_params=params(12),
        name="gather",
        cost_estimate=cost(2.2),
    )(lent, me.reshape(1), grad_blocks, halo_core, halo_far, codes)
    came_back = lax.all_to_all(
        back_points.reshape(slabs, capacity, C), "slab", split_axis=0, concat_axis=0, tiled=True
    )
    point_grads = pl.pallas_call(
        unpack_kernel,
        out_shape=struct(points, C),
        in_specs=[VMEM, VMEM],
        out_specs=VMEM,
        compiler_params=params(12),
        name="unpack",
        cost_estimate=cost(1.7),
    )(came_back.reshape(slabs * capacity, C), dest)

    for bit in range(2, bits):
        if bit > 2:
            kept, sent = halve(kept, arrived, side(bit))
            arrived = swapped(sent, "slab", bit)
        if bit == bits - 2:
            kept = kept + arrived
            step = 0
            while (1 << step) < windows:
                arrived = swapped(kept, "dp", step)
                step += 1
                if (1 << step) < windows:
                    kept = kept + arrived
    share = kept + arrived
    scale = 1.0 / math.sqrt(windows * slabs * voxels)
    return (activated[None], point_grads[None], share * scale)


def solution(mesh):
    return jax.shard_map(
        per_device,
        mesh=mesh,
        in_specs=(
            P("dp", "slab", None),
            P("dp", "slab", None),
            P("dp", "slab"),
            P("dp", "slab"),
            P("dp", "slab", None, None),
            P("dp", "slab", None),
            P(),
            P("dp", "slab", None),
        ),
        out_specs=(P("dp", "slab", None), P("dp", "slab", None), P("slab", None)),
        check_vma=False,
    )
```

```python
import functools
import math

import jax
import jax.numpy as jnp
from jax import lax
from jax.experimental import pallas as pl
from jax.experimental.pallas import tpu as pltpu
from jax.sharding import PartitionSpec as P

C = 128
E = 8
NB = 2
VOX = 512
FACE = E * E
PAD = E + 2
COLS = 9 * C

f32 = jnp.float32
bf16 = jnp.bfloat16
VMEM = pl.BlockSpec(memory_space=pltpu.VMEM)
SMEM = pl.BlockSpec(memory_space=pltpu.SMEM)
ANY = pl.BlockSpec(memory_space=pl.ANY)
HBM = pl.BlockSpec(memory_space=pltpu.HBM)


def params(mib):
    return pltpu.CompilerParams(vmem_limit_bytes=mib << 20)


def cost(microseconds):
    return pl.CostEstimate(flops=int(microseconds * 1e9), bytes_accessed=0, transcendentals=0)


def struct(*shape, dtype=f32):
    return jax.ShapeDtypeStruct(shape, dtype)


def mm(a, b, dims=((1,), (0,))):
    return lax.dot_general(a, b, (dims, ((), ())), preferred_element_type=f32)


def split(value):
    high = value.astype(bf16)
    return high, (value - high.astype(f32)).astype(bf16)


def split3(value):
    high = value.astype(bf16)
    rest = value - high.astype(f32)
    middle = rest.astype(bf16)
    return high, middle, (rest - middle.astype(f32)).astype(bf16)


def iota(shape, dim):
    return lax.broadcasted_iota(jnp.int32, shape, dim)


def pack_kernel(
    slabs, capacity, me_ref, feats_in, owner_in, slot_in, vox_in, out, dest_out, feats, owner, slot, vox, sems
):
    copies = [
        pltpu.make_async_copy(source, target, sems.at[n])
        for n, (source, target) in enumerate(
            ((owner_in, owner), (slot_in, slot), (vox_in, vox), (feats_in, feats))
        )
    ]
    for copy in copies:
        copy.start()
    points = feats.shape[0]
    block = capacity + 8
    for copy in copies[:3]:
        copy.wait()
    target = owner[...]
    onehot = iota((slabs, points), 0) == target
    marks = jnp.where(onehot, 1.0, 0.0).astype(bf16)
    earlier = jnp.where(iota((points, points), 0) < iota((points, points), 1), 1.0, 0.0).astype(bf16)
    counts = mm(marks, earlier)
    rank = jnp.sum(jnp.where(onehot, counts, 0.0), axis=0, keepdims=True).astype(jnp.int32)
    place = target * block + rank
    dest_out[...] = jnp.broadcast_to(target * capacity + rank, dest_out.shape)
    chosen = jnp.where(iota((slabs * block, points), 0) == place, 1.0, 0.0).astype(bf16)
    copies[3].wait()
    parts = jnp.concatenate(split3(feats[...]), axis=1)
    rows = mm(chosen, parts)
    rows = rows[:, :C] + rows[:, C : 2 * C] + rows[:, 2 * C :]
    out[...] = rows.reshape(slabs, block, C)
    code = slot[...] * VOX + vox[...] + 1
    upper = lax.shift_right_logical(code, 5)
    lower = jnp.bitwise_and(code, 31)
    lane = lax.rem(me_ref[0], C // capacity) * capacity + rank
    lanes = jnp.where(iota((C, points), 0) == lane, 1.0, 0.0).astype(bf16)
    nt = ((1,), (1,))
    high = mm(jnp.where(onehot, upper, 0).astype(f32).astype(bf16), lanes, nt)
    low = mm(jnp.where(onehot, lower, 0).astype(f32).astype(bf16), lanes, nt)
    ids = high * 32.0 + low
    out[:, capacity:, :] = jnp.broadcast_to(ids[:, None, :], (slabs, 8, C))


def weights_kernel(taps, backward):
    for i in range(3):
        for jk in range(9):
            high, low = split(taps[i * 9 + jk].T)
            columns = slice(jk * C, (jk + 1) * C)
            backward[i * C : (i + 1) * C, columns] = high
            backward[(3 + i) * C : (4 + i) * C, columns] = high
            backward[(6 + i) * C : (7 + i) * C, columns] = low


def split_taps(taps, forward):
    for i in range(3):
        for jk in range(9):
            high, low = split(taps[i * 9 + jk])
            for part in range(2):
                rows = slice(part * COLS + jk * C, part * COLS + (jk + 1) * C)
                forward[i, rows, :C] = high
                forward[i, rows, C:] = low


def codes_of(ids, chunk, group):
    total = ids[chunk * group]
    for t in range(1, group):
        total = total + ids[chunk * group + t]
    return total


def received(recv, capacity):
    slabs = recv.shape[0]
    rows = recv[:, :capacity, :].reshape(slabs * capacity, C)
    return recv[:, capacity:, :], jnp.concatenate(split(rows), axis=1)


def faces_kernel(capacity, lent, me, recv, to_core, to_far):
    group = C // capacity
    ids, row_parts = received(recv, capacity)
    row = iota((2 * FACE, C), 0)
    number = jnp.where(row < FACE, lent[0] * VOX + row, lent[1] * VOX + VOX - 2 * FACE + row)
    number = number.astype(f32) + 1.0
    hot = []
    for chunk in range(recv.shape[0] // group):
        match = number == codes_of(ids, chunk, group)[:1]
        hot.append(jnp.where(match, 1.0, 0.0).astype(bf16))
    sums = mm(jnp.concatenate(hot, axis=1), row_parts)
    sums = sums[:, :C] + sums[:, C:]
    even = jnp.bitwise_and(me[0], 1) == 0
    to_core[...] = jnp.where(even, sums[FACE:], sums[:FACE])
    to_far[...] = jnp.where(even, sums[:FACE], sums[FACE:])


def sublane(shape):
    return iota(shape, len(shape) - 2)


def plane_versions(first, center, last):
    three = [jnp.concatenate([first[k], center[k], last[k]], axis=0).reshape(PAD, E, C) for k in range(3)]
    z = sublane((PAD, E, C))
    down = pltpu.roll(jnp.where(z == E - 1, three[0], three[1]), 1, 1)
    up = pltpu.roll(jnp.where(z == 0, three[2], three[1]), E - 1, 1)
    return [v.reshape(PAD * E, C) for v in (down, three[1], up)]


def put_columns(columns, rows, versions):
    for k in range(3):
        for j in range(3):
            high, low = split(versions[k][E * j : E * j + FACE])
            at = (3 * j + k) * C
            columns[rows, at : at + C] = high
            columns[rows, COLS + at : COLS + at + C] = low


def load(source, block, stride, offset, size):
    return source[pl.ds(pl.multiple_of(block * stride + offset, E), size), :]


def build_plane(names, b, i, source, stride, offset, limit):
    def piece(j, k, at, size):
        name = jnp.minimum(names[b, 9 * i + 3 * j + k], limit)
        return load(source, name, stride, offset + at, size)

    first = [piece(0, k, FACE - E, E) for k in range(3)]
    center = [piece(1, k, 0, FACE) for k in range(3)]
    last = [piece(2, k, 0, E) for k in range(3)]
    return plane_versions(first, center, last)


def spread_plane(names, b, i, sums, target, stride, offset, limit):
    z = sublane((PAD, E, C))
    three = [s.reshape(PAD, E, C) for s in sums]
    down = pltpu.roll(three[0], E - 1, 1)
    up = pltpu.roll(three[2], 1, 1)
    zero = jnp.zeros_like(down)
    own = three[1] + jnp.where(z < E - 1, down, zero) + jnp.where(z > 0, up, zero)
    values = [jnp.where(z == E - 1, down, zero), own, jnp.where(z == 0, up, zero)]
    for k in range(3):
        value = values[k].reshape(PAD * E, C)
        for j, at, size, start in ((0, FACE - E, E, 0), (1, 0, FACE, E), (2, 0, E, E + FACE)):
            name = jnp.minimum(names[b, 9 * i + 3 * j + k], limit)
            where = pl.ds(pl.multiple_of(name * stride + offset + at, E), size)
            target[where, :] = target[where, :] + value[start : start + size]


def column_sums(back):
    sums = []
    for k in range(3):
        total = None
        for j in range(3):
            around = [back(3 * j + k)]
            if j > 0:
                around.insert(0, jnp.zeros((E * j, C), f32))
            if j < 2:
                around.append(jnp.zeros((E * (2 - j), C), f32))
            value = jnp.concatenate(around, axis=0)
            total = value if total is None else total + value
        sums.append(total)
    return sums


def interior_kernel(
    capacity, names_in, recv, taps_in,
    before, columns, faces, codes_out, forward,
    names, visible, taps, sems,
):
    names_copy = pltpu.make_async_copy(names_in, names, sems.at[0])
    taps_copy = pltpu.make_async_copy(taps_in, taps, sems.at[1])
    names_copy.start()
    taps_copy.start()
    voxels = NB * VOX
    group = C // capacity
    ids, row_parts = received(recv, capacity)
    tiles = []
    for chunk in range(recv.shape[0] // group):
        codes = codes_of(ids, chunk, group)
        codes_out[chunk * 8 : (chunk + 1) * 8, :] = codes
        tiles.append(codes[:1])
    for start in range(0, voxels, C):
        number = iota((C, C), 0).astype(f32) + (start + 1.0)
        hot = [jnp.where(number == tile, 1.0, 0.0).astype(bf16) for tile in tiles]
        sums = mm(jnp.concatenate(hot, axis=1), row_parts)
        visible[start : start + C] = sums[:, :C] + sums[:, C:]
    visible[voxels:] = jnp.zeros((VOX, C), f32)
    for b in range(NB):
        faces[b * FACE : (b + 1) * FACE] = visible[(b + 1) * VOX - FACE : (b + 1) * VOX]
        faces[(NB + b) * FACE : (NB + b + 1) * FACE] = visible[b * VOX : b * VOX + FACE]
    names_copy.wait()
    for b in range(NB):
        for x in range(E):
            rows = slice(b * VOX + x * FACE, b * VOX + (x + 1) * FACE)
            put_columns(columns, rows, build_plane(names, b, 1, visible, VOX, x * FACE, 2))
        if b == 0:
            taps_copy.wait()
            split_taps(taps, forward)
        low, high = b * VOX, (b + 1) * VOX
        total = mm(columns[low:high, :], forward[1])
        before[low:high] = total[:, :C] + total[:, C:]
        total = mm(columns[low : high - FACE, :], forward[0])
        before[low + FACE : high] = before[low + FACE : high] + total[:, :C] + total[:, C:]
        total = mm(columns[low + FACE : high, :], forward[2])
        before[low : high - FACE] = before[low : high - FACE] + total[:, :C] + total[:, C:]


def finish_kernel(
    names_in, me, before, faces, from_core, from_far, forward, backward_in, cotangent_in,
    activated, grads, outer, to_core, to_far,
    names, faces_low, faces_high, pre, cotangent, backward, edge_back, low_grads, high_grads, sems,
):
    copies = [
        pltpu.make_async_copy(names_in, names, sems.at[0]),
        pltpu.make_async_copy(cotangent_in, cotangent, sems.at[1]),
    ]
    for n, i in enumerate((0, 2)):
        for part in (0, 3, 6):
            rows = pl.ds((i + part) * C, C)
            copies.append(
                pltpu.make_async_copy(
                    backward_in.at[rows], backward.at[pl.ds((3 * n + part // 3) * C, C)], sems.at[len(copies)]
                )
            )
    for copy in copies:
        copy.start()
    even = jnp.bitwise_and(me[0], 1) == 0
    none = jnp.zeros((FACE, C), f32)
    faces_low[: 2 * FACE] = faces[: 2 * FACE]
    faces_low[2 * FACE : 3 * FACE] = jnp.where(even, from_far[...], from_core[...])
    faces_low[3 * FACE : 4 * FACE] = none
    faces_low[4 * FACE :] = none
    faces_high[: 2 * FACE] = faces[2 * FACE :]
    faces_high[2 * FACE : 3 * FACE] = none
    faces_high[3 * FACE : 4 * FACE] = jnp.where(even, from_core[...], from_far[...])
    faces_high[4 * FACE :] = none
    low_grads[...] = jnp.zeros_like(low_grads)
    high_grads[...] = jnp.zeros_like(high_grads)
    pre[...] = before[...]
    copies[0].wait()
    for n, (i, x, source) in enumerate(((0, 0, faces_low), (2, E - 1, faces_high))):
        for b in range(NB):
            rows = slice(b * FACE, (b + 1) * FACE)
            put_columns(outer.at[n], rows, build_plane(names, b, i, source, FACE, 0, 4))
        total = mm(outer[n], forward[i])
        total = total[:, :C] + total[:, C:]
        for b in range(NB):
            here = slice(b * VOX + x * FACE, b * VOX + (x + 1) * FACE)
            pre[here] = pre[here] + total[b * FACE : (b + 1) * FACE]
    value = pre[...]
    gate = jax.nn.sigmoid(value)
    activated[...] = value * gate
    copies[1].wait()
    high, low = split(cotangent[...] * gate * (1.0 + value * (1.0 - gate)))
    grads[:, :C] = high
    grads[:, C:] = low
    for copy in copies[2:]:
        copy.wait()
    for n, (i, x, target) in enumerate(((0, 0, low_grads), (2, E - 1, high_grads))):
        both = jnp.concatenate([grads[b * VOX + x * FACE : b * VOX + (x + 1) * FACE, :] for b in range(NB)], axis=0)
        three = jnp.concatenate([both, both[:, :C]], axis=1)
        edge_back[...] = mm(three, backward[3 * n * C : 3 * (n + 1) * C, :])
        for b in range(NB):
            sums = column_sums(lambda jk: edge_back[b * FACE : (b + 1) * FACE, jk * C : (jk + 1) * C])
            spread_plane(names, b, i, sums, target, FACE, 0, 4)
    left = low_grads[2 * FACE : 3 * FACE]
    right = high_grads[3 * FACE : 4 * FACE]
    to_core[...] = jnp.where(even, right, left)
    to_far[...] = jnp.where(even, left, right)


def face_grads(grads, i):
    x = 0 if i == 0 else E - 1
    return jnp.concatenate([grads[(b * E + x) * FACE : (b * E + x + 1) * FACE, :] for b in range(NB)], axis=0)


def shifted_grads(grads, i):
    none = jnp.zeros((FACE, grads.shape[1]), bf16)
    rows = []
    for b in range(NB):
        block = grads[b * VOX : (b + 1) * VOX, :]
        rows += [[block[FACE:], none], [block], [none, block[: VOX - FACE]]][i]
    return jnp.concatenate(rows, axis=0)


def weight_grad_kernel(chunk, pieces, me, columns, outer, grads, kept, sent, ordered):
    tn = ((0,), (0,))
    shifted = [shifted_grads(grads, i) for i in range(3)]
    wide = jnp.concatenate(shifted, axis=1)
    narrow = jnp.concatenate([value[:, :C] for value in shifted], axis=1)
    faces = [face_grads(grads, i) for i in range(3)]
    for start in range(0, COLS, 3 * C):
        high = slice(start, start + 3 * C)
        low = slice(COLS + start, COLS + start + 3 * C)
        term = mm(columns[:, high], wide, tn)
        rest = mm(columns[:, low], narrow, tn)
        for i in range(3):
            value = term[:, 2 * i * C : (2 * i + 1) * C] + term[:, (2 * i + 1) * C : (2 * i + 2) * C]
            value = value + rest[:, i * C : (i + 1) * C]
            if i != 1:
                face = mm(outer[i // 2, :, high], faces[i], tn)
                value = value + face[:, :C] + face[:, C:]
                value = value + mm(outer[i // 2, :, low], faces[i][:, :C], tn)
            ordered[i * COLS + start : i * COLS + start + 3 * C] = value
    first = jnp.bitwise_and(me[0], 1) == 0
    for n, runs in enumerate(pieces):
        for start, size, to in runs:
            start = 2 * n * chunk + start
            even = ordered[start : start + size]
            odd = ordered[start + chunk : start + chunk + size]
            kept[to : to + size] = jnp.where(first, even, odd)
            sent[to : to + size] = jnp.where(first, odd, even)


def halve_kernel(split_at, side, kept, arrived, kept_out, sent_out):
    total, half = kept.shape[0], kept_out.shape[0]
    for start, stop in ((0, split_at), (split_at, total)):
        size = (stop - start) // 2
        to = slice(start // 2, start // 2 + size)
        mine = pl.ds(pl.multiple_of(start + side[0] * size, 8), size)
        other = pl.ds(pl.multiple_of(start + (1 - side[0]) * size, 8), size)
        kept_out[to] = kept[mine, :] + arrived[mine, :]
        sent_out[to] = kept[other, :] + arrived[other, :]


def part_of(kept, arrived, start, size):
    return lax.dynamic_slice_in_dim(kept, start, size, 0) + lax.dynamic_slice_in_dim(arrived, start, size, 0)


def halve(kept, arrived, split_at, side):
    total = kept.shape[0]
    if split_at % 16 == 0 and total % 16 == 0:
        return pl.pallas_call(
            functools.partial(halve_kernel, split_at),
            out_shape=(struct(total // 2, C),) * 2,
            in_specs=[SMEM, VMEM, VMEM],
            out_specs=(VMEM, VMEM),
            compiler_params=params(4),
            name="halve",
            cost_estimate=cost(5),
        )(side.reshape(1), kept, arrived)
    one, two = split_at // 2, (total - split_at) // 2

    def take(which):
        return jnp.concatenate(
            [part_of(kept, arrived, which * one, one), part_of(kept, arrived, split_at + which * two, two)], axis=0
        )

    return take(side), take(1 - side)


def backward_kernel(
    names_in, lent, me, grads, backward_in, halo_core, halo_far, blocks_out,
    names, backward, shifted, back, target, sems,
):
    copies = [
        pltpu.make_async_copy(names_in, names, sems.at[0]),
        pltpu.make_async_copy(backward_in, backward, sems.at[1]),
    ]
    for copy in copies:
        copy.start()
    target[...] = jnp.zeros_like(target)
    shifted[...] = jnp.zeros_like(shifted)
    copies[0].wait()
    for b in range(NB):
        rows = slice(b * VOX, (b + 1) * VOX)
        for i in range(3):
            at = slice(FACE * i, FACE * i + VOX)
            shifted[at, i * C : (i + 1) * C] = grads[rows, :C]
            shifted[at, (3 + i) * C : (4 + i) * C] = grads[rows, C:]
            shifted[at, (6 + i) * C : (7 + i) * C] = grads[rows, :C]
        if b == 0:
            copies[1].wait()
        back[b] = mm(shifted[...], backward[...])
    for b in range(NB):
        for p in range(PAD):
            i = 0 if p == 0 else 2 if p == PAD - 1 else 1
            offset = (VOX - FACE, (p - 1) * FACE, 0)[i]
            rows = slice(p * FACE, (p + 1) * FACE)
            sums = column_sums(lambda jk: back[b, rows, jk * C : (jk + 1) * C])
            spread_plane(names, b, i, sums, target, VOX, offset, 2)
    even = jnp.bitwise_and(me[0], 1) == 0
    left = pl.ds(pl.multiple_of(lent[0] * VOX, VOX), FACE)
    right = pl.ds(pl.multiple_of(lent[1] * VOX, VOX) + VOX - FACE, FACE)
    target[left, :] = target[left, :] + jnp.where(even, halo_far[...], halo_core[...])
    target[right, :] = target[right, :] + jnp.where(even, halo_core[...], halo_far[...])
    blocks_out[...] = target[: NB * VOX]


def gather_kernel(grad_blocks, codes, out):
    voxels = NB * VOX
    parts = jnp.concatenate(split(grad_blocks[...]), axis=1)
    by_row = codes[...].T
    numbers = iota((C, voxels), 1).astype(f32) + 1.0
    for chunk in range(codes.shape[0] // 8):
        match = numbers == by_row[:, chunk * 8 : chunk * 8 + 1]
        rows = mm(jnp.where(match, 1.0, 0.0).astype(bf16), parts)
        out[chunk * C : (chunk + 1) * C] = rows[:, :C] + rows[:, C:]


def pass_kernel(rows, one, two, out):
    del rows, one, two, out


def unpack_kernel(came_back, dest, out):
    places = dest[...].astype(f32).T[:, :1]
    points, slots = out.shape[0], came_back.shape[0]
    chosen = jnp.where(iota((points, slots), 1).astype(f32) == places, 1.0, 0.0).astype(bf16)
    rows = mm(chosen, jnp.concatenate(split3(came_back[...]), axis=1))
    out[...] = rows[:, :C] + rows[:, C : 2 * C] + rows[:, 2 * C :]


def place(slab, order):
    number = 0
    for bit in order:
        number = 2 * number + (slab >> bit & 1)
    return number


def per_device(
    point_feats, owner_slab, block_slot, voxel_index, boundary, neighbours, weight_taps, cotangent
):
    slabs = lax.axis_size("slab")
    windows = lax.axis_size("dp")
    points = point_feats.shape[1]
    capacity = 2 * points // slabs
    bits = slabs.bit_length() - 1
    me = lax.axis_index("slab")
    names = neighbours[0]
    lent = boundary.reshape(2)
    voxels = NB * VOX
    chunk = 27 * C // slabs

    send, dest = pl.pallas_call(
        functools.partial(pack_kernel, slabs, capacity),
        out_shape=(struct(slabs, capacity + 8, C), struct(8, points, dtype=jnp.int32)),
        in_specs=[SMEM] + [HBM] * 4,
        out_specs=(VMEM, VMEM),
        scratch_shapes=[pltpu.VMEM((points, C), f32)]
        + [pltpu.VMEM((1, points), jnp.int32)] * 3
        + [pltpu.SemaphoreType.DMA((4,))],
        compiler_params=params(60),
        name="pack",
        cost_estimate=cost(2),
    )(me.reshape(1), point_feats[0], owner_slab.reshape(1, points), block_slot, voxel_index)
    send, weight_taps = lax.optimization_barrier((send, weight_taps))
    recv = lax.all_to_all(send, "slab", split_axis=0, concat_axis=0, tiled=True)
    backward = pl.pallas_call(
        weights_kernel,
        out_shape=struct(9 * C, COLS, dtype=bf16),
        in_specs=[VMEM],
        out_specs=VMEM,
        compiler_params=params(4),
        name="weights",
        cost_estimate=cost(0.6),
    )(weight_taps)
    recv, backward = lax.optimization_barrier((recv, backward))
    to_core, to_far = pl.pallas_call(
        functools.partial(faces_kernel, capacity),
        out_shape=(struct(FACE, C), struct(FACE, C)),
        in_specs=[SMEM, SMEM, VMEM],
        out_specs=(VMEM,) * 2,
        compiler_params=params(8),
        name="faces",
        cost_estimate=cost(0.8),
    )(lent, me.reshape(1), recv)
    core_pairs = [(i, i ^ 1) for i in range(slabs)]
    far_pairs = [(i, (i - 1 if i % 2 == 0 else i + 1) % slabs) for i in range(slabs)]
    from_core = lax.ppermute(to_core, "slab", core_pairs)
    from_far = lax.ppermute(to_far, "slab", far_pairs)
    before, columns, faces, codes, forward = pl.pallas_call(
        functools.partial(interior_kernel, capacity),
        out_shape=(
            struct(voxels, C),
            struct(voxels, 2 * COLS, dtype=bf16),
            struct(2 * NB * FACE, C),
            struct(slabs * capacity // C * 8, C),
            struct(3, 2 * COLS, 2 * C, dtype=bf16),
        ),
        in_specs=[ANY, VMEM, ANY],
        out_specs=(VMEM,) * 5,
        scratch_shapes=[
            pltpu.SMEM((NB, 27), jnp.int32),
            pltpu.VMEM((3 * VOX, C), f32),
            pltpu.VMEM(weight_taps.shape, f32),
            pltpu.SemaphoreType.DMA((2,)),
        ],
        compiler_params=params(16),
        name="interior",
        cost_estimate=cost(5),
    )(names, recv, weight_taps)
    activated, grads, outer, edge_core, edge_far = pl.pallas_call(
        finish_kernel,
        out_shape=(
            struct(voxels, C),
            struct(voxels, 2 * C, dtype=bf16),
            struct(2, NB * FACE, 2 * COLS, dtype=bf16),
            struct(FACE, C),
            struct(FACE, C),
        ),
        in_specs=[ANY, SMEM] + [VMEM] * 5 + [ANY] * 2,
        out_specs=(VMEM,) * 5,
        scratch_shapes=[
            pltpu.SMEM((NB, 27), jnp.int32),
            pltpu.VMEM((5 * FACE, C), f32),
            pltpu.VMEM((5 * FACE, C), f32),
            pltpu.VMEM((voxels, C), f32),
            pltpu.VMEM((voxels, C), f32),
            pltpu.VMEM((6 * C, COLS), bf16),
            pltpu.VMEM((NB * FACE, COLS), f32),
            pltpu.VMEM((5 * FACE, C), f32),
            pltpu.VMEM((5 * FACE, C), f32),
            pltpu.SemaphoreType.DMA((8,)),
        ],
        compiler_params=params(14),
        name="finish",
        cost_estimate=cost(2.8),
    )(names, me.reshape(1), before, faces, from_core, from_far, forward, backward, cotangent[0])
    cut = -(-chunk // 16) * 8
    rest = list(range(3, bits))
    orders = ([1, 2] + rest, [2, 1] + rest)
    pieces = tuple(
        (
            (0, cut, place(2 * n, orders[0]) * cut),
            (cut, chunk - cut, slabs // 2 * cut + place(2 * n, orders[1]) * (chunk - cut)),
        )
        for n in range(slabs // 2)
    )
    kept, sent = pl.pallas_call(
        functools.partial(weight_grad_kernel, chunk, pieces),
        out_shape=(struct(27 * C // 2, C),) * 2,
        in_specs=[SMEM] + [VMEM] * 3,
        out_specs=(VMEM, VMEM),
        scratch_shapes=[pltpu.VMEM((27 * C, C), f32)],
        compiler_params=params(14),
        name="weight_grad",
        cost_estimate=cost(4),
    )(me.reshape(1), columns, outer, grads)
    def swapped(part, axis, bit):
        size = lax.axis_size(axis)
        return lax.ppermute(part, axis, [(i, i ^ (1 << bit)) for i in range(size)])

    def side(bit):
        return lax.shift_right_logical(me, bit) & 1

    halo_far = lax.ppermute(edge_far, "slab", far_pairs)
    halo_core = lax.ppermute(edge_core, "slab", core_pairs)
    arrived = swapped(sent, "slab", 0)
    mids, sides = slabs // 2 * cut, (side(1), side(2))
    halves = (mids // 2, (kept.shape[0] - mids) // 2)
    sent = [part_of(kept, arrived, (0, mids)[q] + (1 - sides[q]) * halves[q], halves[q]) for q in range(2)]
    sent[0], sent[1], grads, halo_far, halo_core = lax.optimization_barrier(
        (sent[0], sent[1], grads, halo_far, halo_core)
    )
    kept = [part_of(kept, arrived, (0, mids)[q] + sides[q] * halves[q], halves[q]) for q in range(2)]
    arrived = [swapped(sent[q], "slab", (1, 2)[q]) for q in range(2)]
    grad_blocks = pl.pallas_call(
        backward_kernel,
        out_shape=struct(voxels, C),
        in_specs=[ANY, SMEM, SMEM, VMEM, ANY, VMEM, VMEM],
        out_specs=VMEM,
        scratch_shapes=[
            pltpu.SMEM((NB, 27), jnp.int32),
            pltpu.VMEM((9 * C, COLS), bf16),
            pltpu.VMEM((PAD * FACE, 9 * C), bf16),
            pltpu.VMEM((NB, PAD * FACE, COLS), f32),
            pltpu.VMEM((3 * VOX, C), f32),
            pltpu.SemaphoreType.DMA((2,)),
        ],
        compiler_params=params(14),
        name="backward",
        cost_estimate=cost(6.5),
    )(names, lent, me.reshape(1), grads, backward, halo_core, halo_far)
    back_points = pl.pallas_call(
        gather_kernel,
        out_shape=struct(slabs * capacity, C),
        in_specs=[VMEM, VMEM],
        out_specs=VMEM,
        compiler_params=params(12),
        name="gather",
        cost_estimate=cost(2.2),
    )(grad_blocks, codes)
    arrived[0], arrived[1], back_points = lax.optimization_barrier((arrived[0], arrived[1], back_points))
    sides, halves = (side(2), side(1)), [half // 2 for half in halves]
    sent = [part_of(kept[q], arrived[q], (1 - sides[q]) * halves[q], halves[q]) for q in range(2)]
    kept = [part_of(kept[q], arrived[q], sides[q] * halves[q], halves[q]) for q in range(2)]
    back_points = pl.pallas_call(
        pass_kernel,
        out_shape=struct(slabs * capacity, C),
        in_specs=[ANY] * 3,
        out_specs=ANY,
        input_output_aliases={0: 0},
        name="pass",
        cost_estimate=cost(2.2),
    )(back_points, *sent)
    arrived = [swapped(sent[q], "slab", (2, 1)[q]) for q in range(2)]
    came_back = lax.all_to_all(
        back_points.reshape(slabs, capacity, C), "slab", split_axis=0, concat_axis=0, tiled=True
    )
    point_grads = pl.pallas_call(
        unpack_kernel,
        out_shape=struct(points, C),
        in_specs=[VMEM, VMEM],
        out_specs=VMEM,
        compiler_params=params(12),
        name="unpack",
        cost_estimate=cost(1.7),
    )(came_back.reshape(slabs * capacity, C), dest)

    kept = jnp.concatenate([kept[q] + arrived[q] for q in range(2)], axis=0)
    split_at, step = halves[0], 0
    while (1 << step) < windows:
        arrived = swapped(kept, "dp", step)
        step += 1
        if (1 << step) < windows:
            kept = kept + arrived
    for bit in rest:
        kept, sent = halve(kept, arrived, split_at, side(bit))
        arrived = swapped(sent, "slab", bit)
        split_at //= 2
    arrived, point_grads = lax.optimization_barrier((arrived, point_grads))
    share = kept + arrived
    scale = 1.0 / math.sqrt(windows * slabs * voxels)
    return (activated[None], point_grads[None], share * scale)


def solution(mesh):
    return jax.shard_map(
        per_device,
        mesh=mesh,
        in_specs=(
            P("dp", "slab", None),
            P("dp", "slab", None),
            P("dp", "slab"),
            P("dp", "slab"),
            P("dp", "slab", None, None),
            P("dp", "slab", None),
            P(),
            P("dp", "slab", None),
        ),
        out_specs=(P("dp", "slab", None), P("dp", "slab", None), P("slab", None)),
        check_vma=False,
    )
```

```python
import functools
import math

import jax
import jax.numpy as jnp
from jax import lax
from jax.experimental import pallas as pl
from jax.experimental.pallas import tpu as pltpu
from jax.sharding import PartitionSpec as P

C = 128
E = 8
NB = 2
VOX = 512
FACE = E * E
PAD = E + 2
COLS = 9 * C

f32 = jnp.float32
bf16 = jnp.bfloat16
VMEM = pl.BlockSpec(memory_space=pltpu.VMEM)
SMEM = pl.BlockSpec(memory_space=pltpu.SMEM)
ANY = pl.BlockSpec(memory_space=pl.ANY)
HBM = pl.BlockSpec(memory_space=pltpu.HBM)


def params(mib):
    return pltpu.CompilerParams(vmem_limit_bytes=mib << 20)


def cost(microseconds):
    return pl.CostEstimate(flops=int(microseconds * 1e9), bytes_accessed=0, transcendentals=0)


def struct(*shape, dtype=f32):
    return jax.ShapeDtypeStruct(shape, dtype)


def mm(a, b, dims=((1,), (0,))):
    return lax.dot_general(a, b, (dims, ((), ())), preferred_element_type=f32)


def split(value):
    high = value.astype(bf16)
    return high, (value - high.astype(f32)).astype(bf16)


def split3(value):
    high = value.astype(bf16)
    rest = value - high.astype(f32)
    middle = rest.astype(bf16)
    return high, middle, (rest - middle.astype(f32)).astype(bf16)


def iota(shape, dim):
    return lax.broadcasted_iota(jnp.int32, shape, dim)


def pack_kernel(
    slabs, capacity, me_ref, feats_in, owner_in, slot_in, vox_in, out, dest_out, feats, owner, slot, vox, sems
):
    copies = [
        pltpu.make_async_copy(source, target, sems.at[n])
        for n, (source, target) in enumerate(
            ((owner_in, owner), (slot_in, slot), (vox_in, vox), (feats_in, feats))
        )
    ]
    for copy in copies:
        copy.start()
    points = feats.shape[0]
    block = capacity + 8
    for copy in copies[:3]:
        copy.wait()
    target = owner[...]
    onehot = iota((slabs, points), 0) == target
    marks = jnp.where(onehot, 1.0, 0.0).astype(bf16)
    earlier = jnp.where(iota((points, points), 0) < iota((points, points), 1), 1.0, 0.0).astype(bf16)
    counts = mm(marks, earlier)
    rank = jnp.sum(jnp.where(onehot, counts, 0.0), axis=0, keepdims=True).astype(jnp.int32)
    place = target * block + rank
    dest_out[...] = jnp.broadcast_to(target * capacity + rank, dest_out.shape)
    chosen = jnp.where(iota((slabs * block, points), 0) == place, 1.0, 0.0).astype(bf16)
    copies[3].wait()
    parts = jnp.concatenate(split3(feats[...]), axis=1)
    rows = mm(chosen, parts)
    rows = rows[:, :C] + rows[:, C : 2 * C] + rows[:, 2 * C :]
    out[...] = rows.reshape(slabs, block, C)
    code = slot[...] * VOX + vox[...] + 1
    upper = lax.shift_right_logical(code, 5)
    lower = jnp.bitwise_and(code, 31)
    lane = lax.rem(me_ref[0], C // capacity) * capacity + rank
    lanes = jnp.where(iota((C, points), 0) == lane, 1.0, 0.0).astype(bf16)
    nt = ((1,), (1,))
    high = mm(jnp.where(onehot, upper, 0).astype(f32).astype(bf16), lanes, nt)
    low = mm(jnp.where(onehot, lower, 0).astype(f32).astype(bf16), lanes, nt)
    ids = high * 32.0 + low
    out[:, capacity:, :] = jnp.broadcast_to(ids[:, None, :], (slabs, 8, C))


def weights_kernel(taps, backward):
    for i in range(3):
        for jk in range(9):
            high, low = split(taps[i * 9 + jk].T)
            columns = slice(jk * C, (jk + 1) * C)
            backward[i * C : (i + 1) * C, columns] = high
            backward[(3 + i) * C : (4 + i) * C, columns] = high
            backward[(6 + i) * C : (7 + i) * C, columns] = low


def split_taps(taps, forward):
    for i in range(3):
        for jk in range(9):
            high, low = split(taps[i * 9 + jk])
            for part in range(2):
                rows = slice(part * COLS + jk * C, part * COLS + (jk + 1) * C)
                forward[i, rows, :C] = high
                forward[i, rows, C:] = low


def codes_of(ids, chunk, group):
    total = ids[chunk * group]
    for t in range(1, group):
        total = total + ids[chunk * group + t]
    return total


def received(recv, capacity):
    slabs = recv.shape[0]
    rows = recv[:, :capacity, :].reshape(slabs * capacity, C)
    return recv[:, capacity:, :], jnp.concatenate(split(rows), axis=1)


def faces_kernel(capacity, lent, me, recv, to_core, to_far):
    group = C // capacity
    ids, row_parts = received(recv, capacity)
    row = iota((2 * FACE, C), 0)
    number = jnp.where(row < FACE, lent[0] * VOX + row, lent[1] * VOX + VOX - 2 * FACE + row)
    number = number.astype(f32) + 1.0
    hot = []
    for chunk in range(recv.shape[0] // group):
        match = number == codes_of(ids, chunk, group)[:1]
        hot.append(jnp.where(match, 1.0, 0.0).astype(bf16))
    sums = mm(jnp.concatenate(hot, axis=1), row_parts)
    sums = sums[:, :C] + sums[:, C:]
    even = jnp.bitwise_and(me[0], 1) == 0
    to_core[...] = jnp.where(even, sums[FACE:], sums[:FACE])
    to_far[...] = jnp.where(even, sums[:FACE], sums[FACE:])


def sublane(shape):
    return iota(shape, len(shape) - 2)


def plane_versions(first, center, last):
    three = [jnp.concatenate([first[k], center[k], last[k]], axis=0).reshape(PAD, E, C) for k in range(3)]
    z = sublane((PAD, E, C))
    down = pltpu.roll(jnp.where(z == E - 1, three[0], three[1]), 1, 1)
    up = pltpu.roll(jnp.where(z == 0, three[2], three[1]), E - 1, 1)
    return [v.reshape(PAD * E, C) for v in (down, three[1], up)]


def put_columns(columns, rows, versions):
    for k in range(3):
        for j in range(3):
            high, low = split(versions[k][E * j : E * j + FACE])
            at = (3 * j + k) * C
            columns[rows, at : at + C] = high
            columns[rows, COLS + at : COLS + at + C] = low


def load(source, block, stride, offset, size):
    return source[pl.ds(pl.multiple_of(block * stride + offset, E), size), :]


def build_plane(names, b, i, source, stride, offset, limit):
    def piece(j, k, at, size):
        name = jnp.minimum(names[b, 9 * i + 3 * j + k], limit)
        return load(source, name, stride, offset + at, size)

    first = [piece(0, k, FACE - E, E) for k in range(3)]
    center = [piece(1, k, 0, FACE) for k in range(3)]
    last = [piece(2, k, 0, E) for k in range(3)]
    return plane_versions(first, center, last)


def spread_plane(names, b, i, sums, target, stride, offset, limit):
    z = sublane((PAD, E, C))
    three = [s.reshape(PAD, E, C) for s in sums]
    down = pltpu.roll(three[0], E - 1, 1)
    up = pltpu.roll(three[2], 1, 1)
    zero = jnp.zeros_like(down)
    own = three[1] + jnp.where(z < E - 1, down, zero) + jnp.where(z > 0, up, zero)
    values = [jnp.where(z == E - 1, down, zero), own, jnp.where(z == 0, up, zero)]
    for k in range(3):
        value = values[k].reshape(PAD * E, C)
        for j, at, size, start in ((0, FACE - E, E, 0), (1, 0, FACE, E), (2, 0, E, E + FACE)):
            name = jnp.minimum(names[b, 9 * i + 3 * j + k], limit)
            where = pl.ds(pl.multiple_of(name * stride + offset + at, E), size)
            target[where, :] = target[where, :] + value[start : start + size]


def column_sums(back):
    sums = []
    for k in range(3):
        total = None
        for j in range(3):
            around = [back(3 * j + k)]
            if j > 0:
                around.insert(0, jnp.zeros((E * j, C), f32))
            if j < 2:
                around.append(jnp.zeros((E * (2 - j), C), f32))
            value = jnp.concatenate(around, axis=0)
            total = value if total is None else total + value
        sums.append(total)
    return sums


def interior_kernel(
    capacity, names_in, recv, taps_in,
    before, columns, faces, codes_out, forward,
    names, visible, taps, sems,
):
    names_copy = pltpu.make_async_copy(names_in, names, sems.at[0])
    taps_copy = pltpu.make_async_copy(taps_in, taps, sems.at[1])
    names_copy.start()
    taps_copy.start()
    voxels = NB * VOX
    group = C // capacity
    ids, row_parts = received(recv, capacity)
    tiles = []
    for chunk in range(recv.shape[0] // group):
        codes = codes_of(ids, chunk, group)
        codes_out[chunk * 8 : (chunk + 1) * 8, :] = codes
        tiles.append(codes[:1])
    for start in range(0, voxels, C):
        number = iota((C, C), 0).astype(f32) + (start + 1.0)
        hot = [jnp.where(number == tile, 1.0, 0.0).astype(bf16) for tile in tiles]
        sums = mm(jnp.concatenate(hot, axis=1), row_parts)
        visible[start : start + C] = sums[:, :C] + sums[:, C:]
    visible[voxels:] = jnp.zeros((VOX, C), f32)
    for b in range(NB):
        faces[b * FACE : (b + 1) * FACE] = visible[(b + 1) * VOX - FACE : (b + 1) * VOX]
        faces[(NB + b) * FACE : (NB + b + 1) * FACE] = visible[b * VOX : b * VOX + FACE]
    names_copy.wait()
    for b in range(NB):
        for x in range(E):
            rows = slice(b * VOX + x * FACE, b * VOX + (x + 1) * FACE)
            put_columns(columns, rows, build_plane(names, b, 1, visible, VOX, x * FACE, 2))
        if b == 0:
            taps_copy.wait()
            split_taps(taps, forward)
        low, high = b * VOX, (b + 1) * VOX
        total = mm(columns[low:high, :], forward[1])
        before[low:high] = total[:, :C] + total[:, C:]
        total = mm(columns[low : high - FACE, :], forward[0])
        before[low + FACE : high] = before[low + FACE : high] + total[:, :C] + total[:, C:]
        total = mm(columns[low + FACE : high, :], forward[2])
        before[low : high - FACE] = before[low : high - FACE] + total[:, :C] + total[:, C:]


def finish_kernel(
    names_in, me, before, faces, from_core, from_far, forward, backward, cotangent_in,
    activated_out, grads, outer, to_core, to_far,
    names, faces_low, faces_high, pre, cotangent, activated, edge_back, low_grads, high_grads, sems,
):
    copies = [
        pltpu.make_async_copy(names_in, names, sems.at[0]),
        pltpu.make_async_copy(cotangent_in, cotangent, sems.at[1]),
    ]
    for copy in copies:
        copy.start()
    even = jnp.bitwise_and(me[0], 1) == 0
    none = jnp.zeros((FACE, C), f32)
    faces_low[: 2 * FACE] = faces[: 2 * FACE]
    faces_low[2 * FACE : 3 * FACE] = jnp.where(even, from_far[...], from_core[...])
    faces_low[3 * FACE : 4 * FACE] = none
    faces_low[4 * FACE :] = none
    faces_high[: 2 * FACE] = faces[2 * FACE :]
    faces_high[2 * FACE : 3 * FACE] = none
    faces_high[3 * FACE : 4 * FACE] = jnp.where(even, from_core[...], from_far[...])
    faces_high[4 * FACE :] = none
    low_grads[...] = jnp.zeros_like(low_grads)
    high_grads[...] = jnp.zeros_like(high_grads)
    pre[...] = before[...]
    copies[0].wait()
    for n, (i, x, source) in enumerate(((0, 0, faces_low), (2, E - 1, faces_high))):
        for b in range(NB):
            rows = slice(b * FACE, (b + 1) * FACE)
            put_columns(outer.at[n], rows, build_plane(names, b, i, source, FACE, 0, 4))
        total = mm(outer[n], forward[i])
        total = total[:, :C] + total[:, C:]
        for b in range(NB):
            here = slice(b * VOX + x * FACE, b * VOX + (x + 1) * FACE)
            pre[here] = pre[here] + total[b * FACE : (b + 1) * FACE]
    value = pre[...]
    gate = jax.nn.sigmoid(value)
    activated[...] = value * gate
    copies.append(pltpu.make_async_copy(activated, activated_out, sems.at[2]))
    copies[2].start()
    copies[1].wait()
    high, low = split(cotangent[...] * gate * (1.0 + value * (1.0 - gate)))
    grads[:, :C] = high
    grads[:, C:] = low
    for n, (i, x, target) in enumerate(((0, 0, low_grads), (2, E - 1, high_grads))):
        both = jnp.concatenate([grads[b * VOX + x * FACE : b * VOX + (x + 1) * FACE, :] for b in range(NB)], axis=0)
        three = jnp.concatenate([both, both[:, :C]], axis=1)
        matching = jnp.concatenate([backward[(i + part) * C : (i + part + 1) * C, :] for part in (0, 3, 6)], axis=0)
        edge_back[...] = mm(three, matching)
        for b in range(NB):
            sums = column_sums(lambda jk: edge_back[b * FACE : (b + 1) * FACE, jk * C : (jk + 1) * C])
            spread_plane(names, b, i, sums, target, FACE, 0, 4)
    left = low_grads[2 * FACE : 3 * FACE]
    right = high_grads[3 * FACE : 4 * FACE]
    to_core[...] = jnp.where(even, right, left)
    to_far[...] = jnp.where(even, left, right)
    copies[2].wait()


def face_grads(grads, i):
    x = 0 if i == 0 else E - 1
    return jnp.concatenate([grads[(b * E + x) * FACE : (b * E + x + 1) * FACE, :] for b in range(NB)], axis=0)


def shifted_grads(grads, i):
    none = jnp.zeros((FACE, grads.shape[1]), bf16)
    rows = []
    for b in range(NB):
        block = grads[b * VOX : (b + 1) * VOX, :]
        rows += [[block[FACE:], none], [block], [none, block[: VOX - FACE]]][i]
    return jnp.concatenate(rows, axis=0)


def weight_grad_kernel(chunk, pieces, me, columns, outer, grads, kept_a, sent_a, kept_b, sent_b, ordered):
    tn = ((0,), (0,))
    shifted = [shifted_grads(grads, i) for i in range(3)]
    wide = jnp.concatenate(shifted, axis=1)
    narrow = jnp.concatenate([value[:, :C] for value in shifted], axis=1)
    faces = [face_grads(grads, i) for i in range(3)]
    for start in range(0, COLS, 3 * C):
        high = slice(start, start + 3 * C)
        low = slice(COLS + start, COLS + start + 3 * C)
        term = mm(columns[:, high], wide, tn)
        rest = mm(columns[:, low], narrow, tn)
        for i in range(3):
            value = term[:, 2 * i * C : (2 * i + 1) * C] + term[:, (2 * i + 1) * C : (2 * i + 2) * C]
            value = value + rest[:, i * C : (i + 1) * C]
            if i != 1:
                face = mm(outer[i // 2, :, high], faces[i], tn)
                value = value + face[:, :C] + face[:, C:]
                value = value + mm(outer[i // 2, :, low], faces[i][:, :C], tn)
            ordered[i * COLS + start : i * COLS + start + 3 * C] = value
    first = jnp.bitwise_and(me[0], 1) == 0
    for n, runs in enumerate(pieces):
        for (start, size, to), kept, sent in zip(runs, (kept_a, kept_b), (sent_a, sent_b)):
            start = 2 * n * chunk + start
            even = ordered[start : start + size]
            odd = ordered[start + chunk : start + chunk + size]
            kept[to : to + size] = jnp.where(first, even, odd)
            sent[to : to + size] = jnp.where(first, odd, even)


def halve_kernel(split_at, side, kept, arrived, kept_out, sent_out):
    total, half = kept.shape[0], kept_out.shape[0]
    for start, stop in ((0, split_at), (split_at, total)):
        size = (stop - start) // 2
        to = slice(start // 2, start // 2 + size)
        mine = pl.ds(pl.multiple_of(start + side[0] * size, 8), size)
        other = pl.ds(pl.multiple_of(start + (1 - side[0]) * size, 8), size)
        kept_out[to] = kept[mine, :] + arrived[mine, :]
        sent_out[to] = kept[other, :] + arrived[other, :]


def part_of(kept, arrived, start, size):
    return lax.dynamic_slice_in_dim(kept, start, size, 0) + lax.dynamic_slice_in_dim(arrived, start, size, 0)


def halve(kept, arrived, split_at, side):
    total = kept.shape[0]
    if split_at % 16 == 0 and total % 16 == 0:
        return pl.pallas_call(
            functools.partial(halve_kernel, split_at),
            out_shape=(struct(total // 2, C),) * 2,
            in_specs=[SMEM, VMEM, VMEM],
            out_specs=(VMEM, VMEM),
            compiler_params=params(4),
            name="halve",
            cost_estimate=cost(5),
        )(side.reshape(1), kept, arrived)
    one, two = split_at // 2, (total - split_at) // 2

    def take(which):
        return jnp.concatenate(
            [part_of(kept, arrived, which * one, one), part_of(kept, arrived, split_at + which * two, two)], axis=0
        )

    return take(side), take(1 - side)


def backward_kernel(
    names_in, lent, me, grads, backward_in, halo_core, halo_far, blocks_out,
    names, backward, shifted, back, target, sems,
):
    copies = [
        pltpu.make_async_copy(names_in, names, sems.at[0]),
        pltpu.make_async_copy(backward_in, backward, sems.at[1]),
    ]
    for copy in copies:
        copy.start()
    target[...] = jnp.zeros_like(target)
    shifted[...] = jnp.zeros_like(shifted)
    copies[0].wait()
    for b in range(NB):
        rows = slice(b * VOX, (b + 1) * VOX)
        for i in range(3):
            at = slice(FACE * i, FACE * i + VOX)
            shifted[at, i * C : (i + 1) * C] = grads[rows, :C]
            shifted[at, (3 + i) * C : (4 + i) * C] = grads[rows, C:]
            shifted[at, (6 + i) * C : (7 + i) * C] = grads[rows, :C]
        if b == 0:
            copies[1].wait()
        back[b] = mm(shifted[...], backward[...])
    for b in range(NB):
        for p in range(PAD):
            i = 0 if p == 0 else 2 if p == PAD - 1 else 1
            offset = (VOX - FACE, (p - 1) * FACE, 0)[i]
            rows = slice(p * FACE, (p + 1) * FACE)
            sums = column_sums(lambda jk: back[b, rows, jk * C : (jk + 1) * C])
            spread_plane(names, b, i, sums, target, VOX, offset, 2)
    even = jnp.bitwise_and(me[0], 1) == 0
    left = pl.ds(pl.multiple_of(lent[0] * VOX, VOX), FACE)
    right = pl.ds(pl.multiple_of(lent[1] * VOX, VOX) + VOX - FACE, FACE)
    target[left, :] = target[left, :] + jnp.where(even, halo_far[...], halo_core[...])
    target[right, :] = target[right, :] + jnp.where(even, halo_core[...], halo_far[...])
    blocks_out[...] = target[: NB * VOX]


def gather_kernel(grad_blocks, codes, out):
    voxels = NB * VOX
    parts = jnp.concatenate(split(grad_blocks[...]), axis=1)
    by_row = codes[...].T
    numbers = iota((C, voxels), 1).astype(f32) + 1.0
    for chunk in range(codes.shape[0] // 8):
        match = numbers == by_row[:, chunk * 8 : chunk * 8 + 1]
        rows = mm(jnp.where(match, 1.0, 0.0).astype(bf16), parts)
        out[chunk * C : (chunk + 1) * C] = rows[:, :C] + rows[:, C:]


def pass_kernel(rows, one, two, out):
    del rows, one, two, out


def unpack_kernel(came_back, dest, out):
    places = dest[...].astype(f32).T[:, :1]
    points, slots = out.shape[0], came_back.shape[0]
    chosen = jnp.where(iota((points, slots), 1).astype(f32) == places, 1.0, 0.0).astype(bf16)
    rows = mm(chosen, jnp.concatenate(split3(came_back[...]), axis=1))
    out[...] = rows[:, :C] + rows[:, C : 2 * C] + rows[:, 2 * C :]


def place(slab, order):
    number = 0
    for bit in order:
        number = 2 * number + (slab >> bit & 1)
    return number


def per_device(
    point_feats, owner_slab, block_slot, voxel_index, boundary, neighbours, weight_taps, cotangent
):
    slabs = lax.axis_size("slab")
    windows = lax.axis_size("dp")
    points = point_feats.shape[1]
    capacity = 2 * points // slabs
    bits = slabs.bit_length() - 1
    me = lax.axis_index("slab")
    names = neighbours[0]
    lent = boundary.reshape(2)
    voxels = NB * VOX
    chunk = 27 * C // slabs

    send, dest = pl.pallas_call(
        functools.partial(pack_kernel, slabs, capacity),
        out_shape=(struct(slabs, capacity + 8, C), struct(8, points, dtype=jnp.int32)),
        in_specs=[SMEM] + [HBM] * 4,
        out_specs=(VMEM, VMEM),
        scratch_shapes=[pltpu.VMEM((points, C), f32)]
        + [pltpu.VMEM((1, points), jnp.int32)] * 3
        + [pltpu.SemaphoreType.DMA((4,))],
        compiler_params=params(60),
        name="pack",
        cost_estimate=cost(2),
    )(me.reshape(1), point_feats[0], owner_slab.reshape(1, points), block_slot, voxel_index)
    send, weight_taps = lax.optimization_barrier((send, weight_taps))
    recv = lax.all_to_all(send, "slab", split_axis=0, concat_axis=0, tiled=True)
    backward = pl.pallas_call(
        weights_kernel,
        out_shape=struct(9 * C, COLS, dtype=bf16),
        in_specs=[VMEM],
        out_specs=VMEM,
        compiler_params=params(4),
        name="weights",
        cost_estimate=cost(0.6),
    )(weight_taps)
    recv, backward = lax.optimization_barrier((recv, backward))
    to_core, to_far = pl.pallas_call(
        functools.partial(faces_kernel, capacity),
        out_shape=(struct(FACE, C), struct(FACE, C)),
        in_specs=[SMEM, SMEM, VMEM],
        out_specs=(VMEM,) * 2,
        compiler_params=params(8),
        name="faces",
        cost_estimate=cost(0.8),
    )(lent, me.reshape(1), recv)
    core_pairs = [(i, i ^ 1) for i in range(slabs)]
    far_pairs = [(i, (i - 1 if i % 2 == 0 else i + 1) % slabs) for i in range(slabs)]
    from_core = lax.ppermute(to_core, "slab", core_pairs)
    from_far = lax.ppermute(to_far, "slab", far_pairs)
    before, columns, faces, codes, forward = pl.pallas_call(
        functools.partial(interior_kernel, capacity),
        out_shape=(
            struct(voxels, C),
            struct(voxels, 2 * COLS, dtype=bf16),
            struct(2 * NB * FACE, C),
            struct(slabs * capacity // C * 8, C),
            struct(3, 2 * COLS, 2 * C, dtype=bf16),
        ),
        in_specs=[ANY, VMEM, ANY],
        out_specs=(VMEM,) * 5,
        scratch_shapes=[
            pltpu.SMEM((NB, 27), jnp.int32),
            pltpu.VMEM((3 * VOX, C), f32),
            pltpu.VMEM(weight_taps.shape, f32),
            pltpu.SemaphoreType.DMA((2,)),
        ],
        compiler_params=params(16),
        name="interior",
        cost_estimate=cost(5),
    )(names, recv, weight_taps)
    activated, grads, outer, edge_core, edge_far = pl.pallas_call(
        finish_kernel,
        out_shape=(
            struct(voxels, C),
            struct(voxels, 2 * C, dtype=bf16),
            struct(2, NB * FACE, 2 * COLS, dtype=bf16),
            struct(FACE, C),
            struct(FACE, C),
        ),
        in_specs=[ANY, SMEM] + [VMEM] * 6 + [ANY],
        out_specs=(ANY,) + (VMEM,) * 4,
        scratch_shapes=[
            pltpu.SMEM((NB, 27), jnp.int32),
            pltpu.VMEM((5 * FACE, C), f32),
            pltpu.VMEM((5 * FACE, C), f32),
            pltpu.VMEM((voxels, C), f32),
            pltpu.VMEM((voxels, C), f32),
            pltpu.VMEM((voxels, C), f32),
            pltpu.VMEM((NB * FACE, COLS), f32),
            pltpu.VMEM((5 * FACE, C), f32),
            pltpu.VMEM((5 * FACE, C), f32),
            pltpu.SemaphoreType.DMA((3,)),
        ],
        compiler_params=params(14),
        name="finish",
        cost_estimate=cost(2.8),
    )(names, me.reshape(1), before, faces, from_core, from_far, forward, backward, cotangent[0])
    cut = -(-chunk // 16) * 8
    rest = list(range(3, bits))
    orders = ([1, 2] + rest, [2, 1] + rest)
    pieces = tuple(
        (
            (0, cut, place(2 * n, orders[0]) * cut),
            (cut, chunk - cut, place(2 * n, orders[1]) * (chunk - cut)),
        )
        for n in range(slabs // 2)
    )
    sizes = (slabs // 2 * cut, slabs // 2 * (chunk - cut))
    kept_a, sent_a, kept_b, sent_b = pl.pallas_call(
        functools.partial(weight_grad_kernel, chunk, pieces),
        out_shape=(struct(sizes[0], C),) * 2 + (struct(sizes[1], C),) * 2,
        in_specs=[SMEM] + [VMEM] * 3,
        out_specs=(VMEM,) * 4,
        scratch_shapes=[pltpu.VMEM((27 * C, C), f32)],
        compiler_params=params(9),
        name="weight_grad",
        cost_estimate=cost(4),
    )(me.reshape(1), columns, outer, grads)
    def swapped(part, axis, bit):
        size = lax.axis_size(axis)
        return lax.ppermute(part, axis, [(i, i ^ (1 << bit)) for i in range(size)])

    def side(bit):
        return lax.shift_right_logical(me, bit) & 1

    halo_far = lax.ppermute(edge_far, "slab", far_pairs)
    halo_core = lax.ppermute(edge_core, "slab", core_pairs)
    kept, arrived = (kept_a, kept_b), (swapped(sent_a, "slab", 0), swapped(sent_b, "slab", 0))
    sides, halves = (side(1), side(2)), [size // 2 for size in sizes]
    sent = [part_of(kept[q], arrived[q], (1 - sides[q]) * halves[q], halves[q]) for q in range(2)]
    sent[0], sent[1], grads = lax.optimization_barrier((sent[0], sent[1], grads))
    kept = [part_of(kept[q], arrived[q], sides[q] * halves[q], halves[q]) for q in range(2)]
    arrived = [swapped(sent[q], "slab", (1, 2)[q]) for q in range(2)]
    grad_blocks = pl.pallas_call(
        backward_kernel,
        out_shape=struct(voxels, C),
        in_specs=[ANY, SMEM, SMEM, VMEM, ANY, VMEM, VMEM],
        out_specs=VMEM,
        scratch_shapes=[
            pltpu.SMEM((NB, 27), jnp.int32),
            pltpu.VMEM((9 * C, COLS), bf16),
            pltpu.VMEM((PAD * FACE, 9 * C), bf16),
            pltpu.VMEM((NB, PAD * FACE, COLS), f32),
            pltpu.VMEM((3 * VOX, C), f32),
            pltpu.SemaphoreType.DMA((2,)),
        ],
        compiler_params=params(14),
        name="backward",
        cost_estimate=cost(6.5),
    )(names, lent, me.reshape(1), grads, backward, halo_core, halo_far)
    back_points = pl.pallas_call(
        gather_kernel,
        out_shape=struct(slabs * capacity, C),
        in_specs=[VMEM, VMEM],
        out_specs=VMEM,
        compiler_params=params(12),
        name="gather",
        cost_estimate=cost(2.2),
    )(grad_blocks, codes)
    arrived[0], arrived[1], back_points = lax.optimization_barrier((arrived[0], arrived[1], back_points))
    sides, halves = (side(2), side(1)), [half // 2 for half in halves]
    sent = [part_of(kept[q], arrived[q], (1 - sides[q]) * halves[q], halves[q]) for q in range(2)]
    kept = [part_of(kept[q], arrived[q], sides[q] * halves[q], halves[q]) for q in range(2)]
    back_points = pl.pallas_call(
        pass_kernel,
        out_shape=struct(slabs * capacity, C),
        in_specs=[ANY] * 3,
        out_specs=ANY,
        input_output_aliases={0: 0},
        compiler_params=params(1),
        name="pass",
        cost_estimate=cost(2.2),
    )(back_points, *sent)
    arrived = [swapped(sent[q], "slab", (2, 1)[q]) for q in range(2)]
    came_back = lax.all_to_all(
        back_points.reshape(slabs, capacity, C), "slab", split_axis=0, concat_axis=0, tiled=True
    )
    point_grads = pl.pallas_call(
        unpack_kernel,
        out_shape=struct(points, C),
        in_specs=[VMEM, VMEM],
        out_specs=VMEM,
        compiler_params=params(12),
        name="unpack",
        cost_estimate=cost(1.7),
    )(came_back.reshape(slabs * capacity, C), dest)

    kept = jnp.concatenate([kept[q] + arrived[q] for q in range(2)], axis=0)
    split_at, step = halves[0], 0
    while (1 << step) < windows:
        arrived = swapped(kept, "dp", step)
        step += 1
        if (1 << step) < windows:
            kept = kept + arrived
    for bit in rest:
        kept, sent = halve(kept, arrived, split_at, side(bit))
        arrived = swapped(sent, "slab", bit)
        split_at //= 2
    arrived, point_grads = lax.optimization_barrier((arrived, point_grads))
    share = kept + arrived
    scale = 1.0 / math.sqrt(windows * slabs * voxels)
    return (activated[None], point_grads[None], share * scale)


def solution(mesh):
    return jax.shard_map(
        per_device,
        mesh=mesh,
        in_specs=(
            P("dp", "slab", None),
            P("dp", "slab", None),
            P("dp", "slab"),
            P("dp", "slab"),
            P("dp", "slab", None, None),
            P("dp", "slab", None),
            P(),
            P("dp", "slab", None),
        ),
        out_specs=(P("dp", "slab", None), P("dp", "slab", None), P("slab", None)),
        check_vma=False,
    )
```

```python
import functools
import math

import jax
import jax.numpy as jnp
from jax import lax
from jax.experimental import pallas as pl
from jax.experimental.pallas import tpu as pltpu
from jax.sharding import PartitionSpec as P

C = 128
E = 8
NB = 2
VOX = 512
FACE = E * E
PAD = E + 2
COLS = 9 * C

f32 = jnp.float32
bf16 = jnp.bfloat16
VMEM = pl.BlockSpec(memory_space=pltpu.VMEM)
SMEM = pl.BlockSpec(memory_space=pltpu.SMEM)
ANY = pl.BlockSpec(memory_space=pl.ANY)
HBM = pl.BlockSpec(memory_space=pltpu.HBM)


def params(mib):
    return pltpu.CompilerParams(vmem_limit_bytes=mib << 20)


def cost(microseconds):
    return pl.CostEstimate(flops=int(microseconds * 1e9), bytes_accessed=0, transcendentals=0)


def struct(*shape, dtype=f32):
    return jax.ShapeDtypeStruct(shape, dtype)


def mm(a, b, dims=((1,), (0,))):
    return lax.dot_general(a, b, (dims, ((), ())), preferred_element_type=f32)


def split(value):
    high = value.astype(bf16)
    return high, (value - high.astype(f32)).astype(bf16)


def split3(value):
    high = value.astype(bf16)
    rest = value - high.astype(f32)
    middle = rest.astype(bf16)
    return high, middle, (rest - middle.astype(f32)).astype(bf16)


def iota(shape, dim):
    return lax.broadcasted_iota(jnp.int32, shape, dim)


def pack_kernel(
    slabs, capacity, me_ref, feats_in, owner_in, slot_in, vox_in, out, dest_out, feats, owner, slot, vox, sems
):
    copies = [
        pltpu.make_async_copy(source, target, sems.at[n])
        for n, (source, target) in enumerate(
            ((owner_in, owner), (slot_in, slot), (vox_in, vox), (feats_in, feats))
        )
    ]
    for copy in copies:
        copy.start()
    points = feats.shape[0]
    block = capacity + 8
    for copy in copies[:3]:
        copy.wait()
    target = owner[...]
    onehot = iota((slabs, points), 0) == target
    marks = jnp.where(onehot, 1.0, 0.0).astype(bf16)
    earlier = jnp.where(iota((points, points), 0) < iota((points, points), 1), 1.0, 0.0).astype(bf16)
    counts = mm(marks, earlier)
    rank = jnp.sum(jnp.where(onehot, counts, 0.0), axis=0, keepdims=True).astype(jnp.int32)
    place = target * block + rank
    dest_out[...] = jnp.broadcast_to(target * capacity + rank, dest_out.shape)
    chosen = jnp.where(iota((slabs * block, points), 0) == place, 1.0, 0.0).astype(bf16)
    copies[3].wait()
    parts = jnp.concatenate(split3(feats[...]), axis=1)
    rows = mm(chosen, parts)
    rows = rows[:, :C] + rows[:, C : 2 * C] + rows[:, 2 * C :]
    out[...] = rows.reshape(slabs, block, C)
    code = slot[...] * VOX + vox[...] + 1
    upper = lax.shift_right_logical(code, 5)
    lower = jnp.bitwise_and(code, 31)
    lane = lax.rem(me_ref[0], C // capacity) * capacity + rank
    lanes = jnp.where(iota((C, points), 0) == lane, 1.0, 0.0).astype(bf16)
    nt = ((1,), (1,))
    high = mm(jnp.where(onehot, upper, 0).astype(f32).astype(bf16), lanes, nt)
    low = mm(jnp.where(onehot, lower, 0).astype(f32).astype(bf16), lanes, nt)
    ids = high * 32.0 + low
    out[:, capacity:, :] = jnp.broadcast_to(ids[:, None, :], (slabs, 8, C))


def weights_kernel(taps, backward):
    for i in range(3):
        for jk in range(9):
            high, low = split(taps[i * 9 + jk].T)
            columns = slice(jk * C, (jk + 1) * C)
            backward[i * C : (i + 1) * C, columns] = high
            backward[(3 + i) * C : (4 + i) * C, columns] = high
            backward[(6 + i) * C : (7 + i) * C, columns] = low


def split_taps(taps, forward):
    for i in range(3):
        for jk in range(9):
            high, low = split(taps[i * 9 + jk])
            for part in range(2):
                rows = slice(part * COLS + jk * C, part * COLS + (jk + 1) * C)
                forward[i, rows, :C] = high
                forward[i, rows, C:] = low


def codes_of(ids, chunk, group):
    total = ids[chunk * group]
    for t in range(1, group):
        total = total + ids[chunk * group + t]
    return total


def received(recv, capacity):
    slabs = recv.shape[0]
    rows = recv[:, :capacity, :].reshape(slabs * capacity, C)
    return recv[:, capacity:, :], jnp.concatenate(split(rows), axis=1)


def faces_kernel(capacity, lent, me, recv, to_core, to_far):
    group = C // capacity
    ids, row_parts = received(recv, capacity)
    row = iota((2 * FACE, C), 0)
    number = jnp.where(row < FACE, lent[0] * VOX + row, lent[1] * VOX + VOX - 2 * FACE + row)
    number = number.astype(f32) + 1.0
    hot = []
    for chunk in range(recv.shape[0] // group):
        match = number == codes_of(ids, chunk, group)[:1]
        hot.append(jnp.where(match, 1.0, 0.0).astype(bf16))
    sums = mm(jnp.concatenate(hot, axis=1), row_parts)
    sums = sums[:, :C] + sums[:, C:]
    even = jnp.bitwise_and(me[0], 1) == 0
    to_core[...] = jnp.where(even, sums[FACE:], sums[:FACE])
    to_far[...] = jnp.where(even, sums[:FACE], sums[FACE:])


def sublane(shape):
    return iota(shape, len(shape) - 2)


def plane_versions(first, center, last):
    three = [jnp.concatenate([first[k], center[k], last[k]], axis=0).reshape(PAD, E, C) for k in range(3)]
    z = sublane((PAD, E, C))
    down = pltpu.roll(jnp.where(z == E - 1, three[0], three[1]), 1, 1)
    up = pltpu.roll(jnp.where(z == 0, three[2], three[1]), E - 1, 1)
    return [v.reshape(PAD * E, C) for v in (down, three[1], up)]


def put_columns(columns, rows, versions):
    for k in range(3):
        for j in range(3):
            high, low = split(versions[k][E * j : E * j + FACE])
            at = (3 * j + k) * C
            columns[rows, at : at + C] = high
            columns[rows, COLS + at : COLS + at + C] = low


def load(source, block, stride, offset, size):
    return source[pl.ds(pl.multiple_of(block * stride + offset, E), size), :]


def build_plane(names, b, i, source, stride, offset, limit):
    def piece(j, k, at, size):
        name = jnp.minimum(names[b, 9 * i + 3 * j + k], limit)
        return load(source, name, stride, offset + at, size)

    first = [piece(0, k, FACE - E, E) for k in range(3)]
    center = [piece(1, k, 0, FACE) for k in range(3)]
    last = [piece(2, k, 0, E) for k in range(3)]
    return plane_versions(first, center, last)


def spread_plane(names, b, i, sums, target, stride, offset, limit):
    z = sublane((PAD, E, C))
    three = [s.reshape(PAD, E, C) for s in sums]
    down = pltpu.roll(three[0], E - 1, 1)
    up = pltpu.roll(three[2], 1, 1)
    zero = jnp.zeros_like(down)
    own = three[1] + jnp.where(z < E - 1, down, zero) + jnp.where(z > 0, up, zero)
    values = [jnp.where(z == E - 1, down, zero), own, jnp.where(z == 0, up, zero)]
    for k in range(3):
        value = values[k].reshape(PAD * E, C)
        for j, at, size, start in ((0, FACE - E, E, 0), (1, 0, FACE, E), (2, 0, E, E + FACE)):
            name = jnp.minimum(names[b, 9 * i + 3 * j + k], limit)
            where = pl.ds(pl.multiple_of(name * stride + offset + at, E), size)
            target[where, :] = target[where, :] + value[start : start + size]


def column_sums(back):
    sums = []
    for k in range(3):
        total = None
        for j in range(3):
            around = [back(3 * j + k)]
            if j > 0:
                around.insert(0, jnp.zeros((E * j, C), f32))
            if j < 2:
                around.append(jnp.zeros((E * (2 - j), C), f32))
            value = jnp.concatenate(around, axis=0)
            total = value if total is None else total + value
        sums.append(total)
    return sums


def interior_kernel(
    capacity, names_in, recv, taps_in,
    before, columns, faces, codes_out, forward,
    names, visible, taps, sems,
):
    names_copy = pltpu.make_async_copy(names_in, names, sems.at[0])
    taps_copy = pltpu.make_async_copy(taps_in, taps, sems.at[1])
    names_copy.start()
    taps_copy.start()
    voxels = NB * VOX
    group = C // capacity
    ids, row_parts = received(recv, capacity)
    tiles = []
    for chunk in range(recv.shape[0] // group):
        codes = codes_of(ids, chunk, group)
        codes_out[chunk * 8 : (chunk + 1) * 8, :] = codes
        tiles.append(codes[:1])
    for start in range(0, voxels, C):
        number = iota((C, C), 0).astype(f32) + (start + 1.0)
        hot = [jnp.where(number == tile, 1.0, 0.0).astype(bf16) for tile in tiles]
        sums = mm(jnp.concatenate(hot, axis=1), row_parts)
        visible[start : start + C] = sums[:, :C] + sums[:, C:]
    visible[voxels:] = jnp.zeros((VOX, C), f32)
    for b in range(NB):
        faces[b * FACE : (b + 1) * FACE] = visible[(b + 1) * VOX - FACE : (b + 1) * VOX]
        faces[(NB + b) * FACE : (NB + b + 1) * FACE] = visible[b * VOX : b * VOX + FACE]
    names_copy.wait()
    for b in range(NB):
        for x in range(E):
            rows = slice(b * VOX + x * FACE, b * VOX + (x + 1) * FACE)
            put_columns(columns, rows, build_plane(names, b, 1, visible, VOX, x * FACE, 2))
        if b == 0:
            taps_copy.wait()
            split_taps(taps, forward)
        low, high = b * VOX, (b + 1) * VOX
        total = mm(columns[low:high, :], forward[1])
        before[low:high] = total[:, :C] + total[:, C:]
        total = mm(columns[low : high - FACE, :], forward[0])
        before[low + FACE : high] = before[low + FACE : high] + total[:, :C] + total[:, C:]
        total = mm(columns[low + FACE : high, :], forward[2])
        before[low : high - FACE] = before[low : high - FACE] + total[:, :C] + total[:, C:]


def finish_kernel(
    names_in, me, before, faces, from_core, from_far, forward, backward, cotangent_in,
    activated_out, grads, outer, to_core, to_far,
    names, faces_low, faces_high, pre, cotangent, activated, edge_back, low_grads, high_grads, sems,
):
    copies = [
        pltpu.make_async_copy(names_in, names, sems.at[0]),
        pltpu.make_async_copy(cotangent_in, cotangent, sems.at[1]),
    ]
    for copy in copies:
        copy.start()
    even = jnp.bitwise_and(me[0], 1) == 0
    none = jnp.zeros((FACE, C), f32)
    faces_low[: 2 * FACE] = faces[: 2 * FACE]
    faces_low[2 * FACE : 3 * FACE] = jnp.where(even, from_far[...], from_core[...])
    faces_low[3 * FACE : 4 * FACE] = none
    faces_low[4 * FACE :] = none
    faces_high[: 2 * FACE] = faces[2 * FACE :]
    faces_high[2 * FACE : 3 * FACE] = none
    faces_high[3 * FACE : 4 * FACE] = jnp.where(even, from_core[...], from_far[...])
    faces_high[4 * FACE :] = none
    low_grads[...] = jnp.zeros_like(low_grads)
    high_grads[...] = jnp.zeros_like(high_grads)
    pre[...] = before[...]
    copies[0].wait()
    for n, (i, x, source) in enumerate(((0, 0, faces_low), (2, E - 1, faces_high))):
        for b in range(NB):
            rows = slice(b * FACE, (b + 1) * FACE)
            put_columns(outer.at[n], rows, build_plane(names, b, i, source, FACE, 0, 4))
        total = mm(outer[n], forward[i])
        total = total[:, :C] + total[:, C:]
        for b in range(NB):
            here = slice(b * VOX + x * FACE, b * VOX + (x + 1) * FACE)
            pre[here] = pre[here] + total[b * FACE : (b + 1) * FACE]
    value = pre[...]
    gate = jax.nn.sigmoid(value)
    activated[...] = value * gate
    copies.append(pltpu.make_async_copy(activated, activated_out, sems.at[2]))
    copies[2].start()
    copies[1].wait()
    high, low = split(cotangent[...] * gate * (1.0 + value * (1.0 - gate)))
    grads[:, :C] = high
    grads[:, C:] = low
    for n, (i, x, target) in enumerate(((0, 0, low_grads), (2, E - 1, high_grads))):
        both = jnp.concatenate([grads[b * VOX + x * FACE : b * VOX + (x + 1) * FACE, :] for b in range(NB)], axis=0)
        three = jnp.concatenate([both, both[:, :C]], axis=1)
        matching = jnp.concatenate([backward[(i + part) * C : (i + part + 1) * C, :] for part in (0, 3, 6)], axis=0)
        edge_back[...] = mm(three, matching)
        for b in range(NB):
            sums = column_sums(lambda jk: edge_back[b * FACE : (b + 1) * FACE, jk * C : (jk + 1) * C])
            spread_plane(names, b, i, sums, target, FACE, 0, 4)
    left = low_grads[2 * FACE : 3 * FACE]
    right = high_grads[3 * FACE : 4 * FACE]
    to_core[...] = jnp.where(even, right, left)
    to_far[...] = jnp.where(even, left, right)
    copies[2].wait()


def face_grads(grads, i):
    x = 0 if i == 0 else E - 1
    return jnp.concatenate([grads[(b * E + x) * FACE : (b * E + x + 1) * FACE, :] for b in range(NB)], axis=0)


def shifted_grads(grads, i):
    none = jnp.zeros((FACE, grads.shape[1]), bf16)
    rows = []
    for b in range(NB):
        block = grads[b * VOX : (b + 1) * VOX, :]
        rows += [[block[FACE:], none], [block], [none, block[: VOX - FACE]]][i]
    return jnp.concatenate(rows, axis=0)


def weight_grad_kernel(chunk, pieces, me, columns, outer, grads, kept_a, sent_a, kept_b, sent_b, ordered):
    tn = ((0,), (0,))
    shifted = [shifted_grads(grads, i) for i in range(3)]
    wide = jnp.concatenate(shifted, axis=1)
    narrow = jnp.concatenate([value[:, :C] for value in shifted], axis=1)
    faces = [face_grads(grads, i) for i in range(3)]
    for start in range(0, COLS, 3 * C):
        high = slice(start, start + 3 * C)
        low = slice(COLS + start, COLS + start + 3 * C)
        term = mm(columns[:, high], wide, tn)
        rest = mm(columns[:, low], narrow, tn)
        for i in range(3):
            value = term[:, 2 * i * C : (2 * i + 1) * C] + term[:, (2 * i + 1) * C : (2 * i + 2) * C]
            value = value + rest[:, i * C : (i + 1) * C]
            if i != 1:
                face = mm(outer[i // 2, :, high], faces[i], tn)
                value = value + face[:, :C] + face[:, C:]
                value = value + mm(outer[i // 2, :, low], faces[i][:, :C], tn)
            ordered[i * COLS + start : i * COLS + start + 3 * C] = value
    first = jnp.bitwise_and(me[0], 1) == 0
    for n, runs in enumerate(pieces):
        for (start, size, to), kept, sent in zip(runs, (kept_a, kept_b), (sent_a, sent_b)):
            start = 2 * n * chunk + start
            even = ordered[start : start + size]
            odd = ordered[start + chunk : start + chunk + size]
            kept[to : to + size] = jnp.where(first, even, odd)
            sent[to : to + size] = jnp.where(first, odd, even)


def halve_kernel(split_at, side, kept, arrived, kept_out, sent_out):
    total, half = kept.shape[0], kept_out.shape[0]
    for start, stop in ((0, split_at), (split_at, total)):
        size = (stop - start) // 2
        to = slice(start // 2, start // 2 + size)
        mine = pl.ds(pl.multiple_of(start + side[0] * size, 8), size)
        other = pl.ds(pl.multiple_of(start + (1 - side[0]) * size, 8), size)
        kept_out[to] = kept[mine, :] + arrived[mine, :]
        sent_out[to] = kept[other, :] + arrived[other, :]


def part_of(kept, arrived, start, size):
    return lax.dynamic_slice_in_dim(kept, start, size, 0) + lax.dynamic_slice_in_dim(arrived, start, size, 0)


def halve(kept, arrived, split_at, side):
    total = kept.shape[0]
    if split_at % 16 == 0 and total % 16 == 0:
        return pl.pallas_call(
            functools.partial(halve_kernel, split_at),
            out_shape=(struct(total // 2, C),) * 2,
            in_specs=[SMEM, VMEM, VMEM],
            out_specs=(VMEM, VMEM),
            compiler_params=params(4),
            name="halve",
            cost_estimate=cost(5),
        )(side.reshape(1), kept, arrived)
    one, two = split_at // 2, (total - split_at) // 2

    def take(which):
        return jnp.concatenate(
            [part_of(kept, arrived, which * one, one), part_of(kept, arrived, split_at + which * two, two)], axis=0
        )

    return take(side), take(1 - side)


def backward_kernel(
    names_in, lent, me, grads, backward, halo_core, halo_far, blocks_out,
    names, shifted, back, target, sem,
):
    names_copy = pltpu.make_async_copy(names_in, names, sem)
    names_copy.start()
    target[...] = jnp.zeros_like(target)
    shifted[...] = jnp.zeros_like(shifted)
    for b in range(NB):
        rows = slice(b * VOX, (b + 1) * VOX)
        for i in range(3):
            at = slice(FACE * i, FACE * i + VOX)
            shifted[at, i * C : (i + 1) * C] = grads[rows, :C]
            shifted[at, (3 + i) * C : (4 + i) * C] = grads[rows, C:]
            shifted[at, (6 + i) * C : (7 + i) * C] = grads[rows, :C]
        back[b] = mm(shifted[...], backward[...])
    names_copy.wait()
    for b in range(NB):
        for p in range(PAD):
            i = 0 if p == 0 else 2 if p == PAD - 1 else 1
            offset = (VOX - FACE, (p - 1) * FACE, 0)[i]
            rows = slice(p * FACE, (p + 1) * FACE)
            sums = column_sums(lambda jk: back[b, rows, jk * C : (jk + 1) * C])
            spread_plane(names, b, i, sums, target, VOX, offset, 2)
    even = jnp.bitwise_and(me[0], 1) == 0
    left = pl.ds(pl.multiple_of(lent[0] * VOX, VOX), FACE)
    right = pl.ds(pl.multiple_of(lent[1] * VOX, VOX) + VOX - FACE, FACE)
    target[left, :] = target[left, :] + jnp.where(even, halo_far[...], halo_core[...])
    target[right, :] = target[right, :] + jnp.where(even, halo_core[...], halo_far[...])
    blocks_out[...] = target[: NB * VOX]


def gather_kernel(grad_blocks, codes, out):
    voxels = NB * VOX
    parts = jnp.concatenate(split(grad_blocks[...]), axis=1)
    by_row = codes[...].T
    numbers = iota((C, voxels), 1).astype(f32) + 1.0
    for chunk in range(codes.shape[0] // 8):
        match = numbers == by_row[:, chunk * 8 : chunk * 8 + 1]
        rows = mm(jnp.where(match, 1.0, 0.0).astype(bf16), parts)
        out[chunk * C : (chunk + 1) * C] = rows[:, :C] + rows[:, C:]


def pass_kernel(rows, one, two, out):
    del rows, one, two, out


def unpack_kernel(came_back, dest, out):
    places = dest[...].astype(f32).T[:, :1]
    points, slots = out.shape[0], came_back.shape[0]
    chosen = jnp.where(iota((points, slots), 1).astype(f32) == places, 1.0, 0.0).astype(bf16)
    rows = mm(chosen, jnp.concatenate(split3(came_back[...]), axis=1))
    out[...] = rows[:, :C] + rows[:, C : 2 * C] + rows[:, 2 * C :]


def place(slab, order):
    number = 0
    for bit in order:
        number = 2 * number + (slab >> bit & 1)
    return number


def per_device(
    point_feats, owner_slab, block_slot, voxel_index, boundary, neighbours, weight_taps, cotangent
):
    slabs = lax.axis_size("slab")
    windows = lax.axis_size("dp")
    points = point_feats.shape[1]
    capacity = 2 * points // slabs
    bits = slabs.bit_length() - 1
    me = lax.axis_index("slab")
    names = neighbours[0]
    lent = boundary.reshape(2)
    voxels = NB * VOX
    chunk = 27 * C // slabs

    send, dest = pl.pallas_call(
        functools.partial(pack_kernel, slabs, capacity),
        out_shape=(struct(slabs, capacity + 8, C), struct(8, points, dtype=jnp.int32)),
        in_specs=[SMEM] + [HBM] * 4,
        out_specs=(VMEM, VMEM),
        scratch_shapes=[pltpu.VMEM((points, C), f32)]
        + [pltpu.VMEM((1, points), jnp.int32)] * 3
        + [pltpu.SemaphoreType.DMA((4,))],
        compiler_params=params(60),
        name="pack",
        cost_estimate=cost(2),
    )(me.reshape(1), point_feats[0], owner_slab.reshape(1, points), block_slot, voxel_index)
    send, weight_taps = lax.optimization_barrier((send, weight_taps))
    recv = lax.all_to_all(send, "slab", split_axis=0, concat_axis=0, tiled=True)
    backward = pl.pallas_call(
        weights_kernel,
        out_shape=struct(9 * C, COLS, dtype=bf16),
        in_specs=[VMEM],
        out_specs=VMEM,
        compiler_params=params(4),
        name="weights",
        cost_estimate=cost(0.6),
    )(weight_taps)
    recv, backward = lax.optimization_barrier((recv, backward))
    to_core, to_far = pl.pallas_call(
        functools.partial(faces_kernel, capacity),
        out_shape=(struct(FACE, C), struct(FACE, C)),
        in_specs=[SMEM, SMEM, VMEM],
        out_specs=(VMEM,) * 2,
        compiler_params=params(8),
        name="faces",
        cost_estimate=cost(0.8),
    )(lent, me.reshape(1), recv)
    core_pairs = [(i, i ^ 1) for i in range(slabs)]
    far_pairs = [(i, (i - 1 if i % 2 == 0 else i + 1) % slabs) for i in range(slabs)]
    from_core = lax.ppermute(to_core, "slab", core_pairs)
    from_far = lax.ppermute(to_far, "slab", far_pairs)
    before, columns, faces, codes, forward = pl.pallas_call(
        functools.partial(interior_kernel, capacity),
        out_shape=(
            struct(voxels, C),
            struct(voxels, 2 * COLS, dtype=bf16),
            struct(2 * NB * FACE, C),
            struct(slabs * capacity // C * 8, C),
            struct(3, 2 * COLS, 2 * C, dtype=bf16),
        ),
        in_specs=[ANY, VMEM, ANY],
        out_specs=(VMEM,) * 5,
        scratch_shapes=[
            pltpu.SMEM((NB, 27), jnp.int32),
            pltpu.VMEM((3 * VOX, C), f32),
            pltpu.VMEM(weight_taps.shape, f32),
            pltpu.SemaphoreType.DMA((2,)),
        ],
        compiler_params=params(16),
        name="interior",
        cost_estimate=cost(5),
    )(names, recv, weight_taps)
    activated, grads, outer, edge_core, edge_far = pl.pallas_call(
        finish_kernel,
        out_shape=(
            struct(voxels, C),
            struct(voxels, 2 * C, dtype=bf16),
            struct(2, NB * FACE, 2 * COLS, dtype=bf16),
            struct(FACE, C),
            struct(FACE, C),
        ),
        in_specs=[ANY, SMEM] + [VMEM] * 6 + [ANY],
        out_specs=(ANY,) + (VMEM,) * 4,
        scratch_shapes=[
            pltpu.SMEM((NB, 27), jnp.int32),
            pltpu.VMEM((5 * FACE, C), f32),
            pltpu.VMEM((5 * FACE, C), f32),
            pltpu.VMEM((voxels, C), f32),
            pltpu.VMEM((voxels, C), f32),
            pltpu.VMEM((voxels, C), f32),
            pltpu.VMEM((NB * FACE, COLS), f32),
            pltpu.VMEM((5 * FACE, C), f32),
            pltpu.VMEM((5 * FACE, C), f32),
            pltpu.SemaphoreType.DMA((3,)),
        ],
        compiler_params=params(14),
        name="finish",
        cost_estimate=cost(2.8),
    )(names, me.reshape(1), before, faces, from_core, from_far, forward, backward, cotangent[0])
    cut = -(-chunk // 16) * 8
    rest = list(range(3, bits))
    orders = ([1, 2] + rest, [2, 1] + rest)
    pieces = tuple(
        (
            (0, cut, place(2 * n, orders[0]) * cut),
            (cut, chunk - cut, place(2 * n, orders[1]) * (chunk - cut)),
        )
        for n in range(slabs // 2)
    )
    sizes = (slabs // 2 * cut, slabs // 2 * (chunk - cut))
    kept_a, sent_a, kept_b, sent_b = pl.pallas_call(
        functools.partial(weight_grad_kernel, chunk, pieces),
        out_shape=(struct(sizes[0], C),) * 2 + (struct(sizes[1], C),) * 2,
        in_specs=[SMEM] + [VMEM] * 3,
        out_specs=(VMEM,) * 4,
        scratch_shapes=[pltpu.VMEM((27 * C, C), f32)],
        compiler_params=params(9),
        name="weight_grad",
        cost_estimate=cost(4),
    )(me.reshape(1), columns, outer, grads)
    def swapped(part, axis, bit):
        size = lax.axis_size(axis)
        return lax.ppermute(part, axis, [(i, i ^ (1 << bit)) for i in range(size)])

    def side(bit):
        return lax.shift_right_logical(me, bit) & 1

    halo_far = lax.ppermute(edge_far, "slab", far_pairs)
    halo_core = lax.ppermute(edge_core, "slab", core_pairs)
    kept, arrived = (kept_a, kept_b), (swapped(sent_a, "slab", 0), swapped(sent_b, "slab", 0))
    sides, halves = (side(1), side(2)), [size // 2 for size in sizes]
    sent = [part_of(kept[q], arrived[q], (1 - sides[q]) * halves[q], halves[q]) for q in range(2)]
    sent[0], sent[1], grads = lax.optimization_barrier((sent[0], sent[1], grads))
    kept = [part_of(kept[q], arrived[q], sides[q] * halves[q], halves[q]) for q in range(2)]
    arrived = [swapped(sent[q], "slab", (1, 2)[q]) for q in range(2)]
    grad_blocks = pl.pallas_call(
        backward_kernel,
        out_shape=struct(voxels, C),
        in_specs=[ANY, SMEM, SMEM] + [VMEM] * 4,
        out_specs=VMEM,
        scratch_shapes=[
            pltpu.SMEM((NB, 27), jnp.int32),
            pltpu.VMEM((PAD * FACE, 9 * C), bf16),
            pltpu.VMEM((NB, PAD * FACE, COLS), f32),
            pltpu.VMEM((3 * VOX, C), f32),
            pltpu.SemaphoreType.DMA,
        ],
        compiler_params=params(14),
        name="backward",
        cost_estimate=cost(6.5),
    )(names, lent, me.reshape(1), grads, backward, halo_core, halo_far)
    back_points = pl.pallas_call(
        gather_kernel,
        out_shape=struct(slabs * capacity, C),
        in_specs=[VMEM, VMEM],
        out_specs=VMEM,
        compiler_params=params(12),
        name="gather",
        cost_estimate=cost(2.2),
    )(grad_blocks, codes)
    arrived[0], arrived[1], back_points = lax.optimization_barrier((arrived[0], arrived[1], back_points))
    sides, halves = (side(2), side(1)), [half // 2 for half in halves]
    sent = [part_of(kept[q], arrived[q], (1 - sides[q]) * halves[q], halves[q]) for q in range(2)]
    kept = [part_of(kept[q], arrived[q], sides[q] * halves[q], halves[q]) for q in range(2)]
    back_points = pl.pallas_call(
        pass_kernel,
        out_shape=struct(slabs * capacity, C),
        in_specs=[ANY] * 3,
        out_specs=ANY,
        input_output_aliases={0: 0},
        name="pass",
        cost_estimate=cost(2.2),
    )(back_points, *sent)
    arrived = [swapped(sent[q], "slab", (2, 1)[q]) for q in range(2)]
    came_back = lax.all_to_all(
        back_points.reshape(slabs, capacity, C), "slab", split_axis=0, concat_axis=0, tiled=True
    )
    point_grads = pl.pallas_call(
        unpack_kernel,
        out_shape=struct(points, C),
        in_specs=[VMEM, VMEM],
        out_specs=VMEM,
        compiler_params=params(12),
        name="unpack",
        cost_estimate=cost(1.7),
    )(came_back.reshape(slabs * capacity, C), dest)

    kept = jnp.concatenate([kept[q] + arrived[q] for q in range(2)], axis=0)
    split_at, step = halves[0], 0
    while (1 << step) < windows:
        arrived = swapped(kept, "dp", step)
        step += 1
        if (1 << step) < windows:
            kept = kept + arrived
    for bit in rest:
        kept, sent = halve(kept, arrived, split_at, side(bit))
        arrived = swapped(sent, "slab", bit)
        split_at //= 2
    arrived, point_grads = lax.optimization_barrier((arrived, point_grads))
    share = kept + arrived
    scale = 1.0 / math.sqrt(windows * slabs * voxels)
    return (activated[None], point_grads[None], share * scale)


def solution(mesh):
    return jax.shard_map(
        per_device,
        mesh=mesh,
        in_specs=(
            P("dp", "slab", None),
            P("dp", "slab", None),
            P("dp", "slab"),
            P("dp", "slab"),
            P("dp", "slab", None, None),
            P("dp", "slab", None),
            P(),
            P("dp", "slab", None),
        ),
        out_specs=(P("dp", "slab", None), P("dp", "slab", None), P("slab", None)),
        check_vma=False,
    )
```

```python
import functools
import math

import jax
import jax.numpy as jnp
from jax import lax
from jax.experimental import pallas as pl
from jax.experimental.pallas import tpu as pltpu
from jax.sharding import PartitionSpec as P

C = 128
E = 8
NB = 2
VOX = 512
FACE = E * E
PAD = E + 2
COLS = 9 * C

f32 = jnp.float32
bf16 = jnp.bfloat16
VMEM = pl.BlockSpec(memory_space=pltpu.VMEM)
SMEM = pl.BlockSpec(memory_space=pltpu.SMEM)
ANY = pl.BlockSpec(memory_space=pl.ANY)
HBM = pl.BlockSpec(memory_space=pltpu.HBM)


def params(mib):
    return pltpu.CompilerParams(vmem_limit_bytes=mib << 20)


def cost(microseconds):
    return pl.CostEstimate(flops=int(microseconds * 1e9), bytes_accessed=0, transcendentals=0)


def struct(*shape, dtype=f32):
    return jax.ShapeDtypeStruct(shape, dtype)


def mm(a, b, dims=((1,), (0,))):
    return lax.dot_general(a, b, (dims, ((), ())), preferred_element_type=f32)


def split(value):
    high = value.astype(bf16)
    return high, (value - high.astype(f32)).astype(bf16)


def iota(shape, dim):
    return lax.broadcasted_iota(jnp.int32, shape, dim)


def pack_kernel(
    slabs, capacity, me_ref, feats_in, owner_in, slot_in, vox_in, out, dest_out, feats, owner, slot, vox, sems
):
    copies = [
        pltpu.make_async_copy(source, target, sems.at[n])
        for n, (source, target) in enumerate(
            ((owner_in, owner), (slot_in, slot), (vox_in, vox), (feats_in, feats))
        )
    ]
    for copy in copies:
        copy.start()
    points = feats.shape[0]
    block = capacity + 8
    for copy in copies[:3]:
        copy.wait()
    target = owner[...]
    onehot = iota((slabs, points), 0) == target
    marks = jnp.where(onehot, 1.0, 0.0).astype(bf16)
    earlier = jnp.where(iota((points, points), 0) < iota((points, points), 1), 1.0, 0.0).astype(bf16)
    counts = mm(marks, earlier)
    rank = jnp.sum(jnp.where(onehot, counts, 0.0), axis=0, keepdims=True).astype(jnp.int32)
    place = target * block + rank
    dest_out[...] = jnp.broadcast_to(target * capacity + rank, dest_out.shape)
    chosen = jnp.where(iota((slabs * block, points), 0) == place, 1.0, 0.0).astype(bf16)
    copies[3].wait()
    parts = jnp.concatenate(split(feats[...]), axis=1)
    rows = mm(chosen, parts)
    rows = rows[:, :C] + rows[:, C:]
    out[...] = rows.reshape(slabs, block, C)
    code = slot[...] * VOX + vox[...] + 1
    upper = lax.shift_right_logical(code, 5)
    lower = jnp.bitwise_and(code, 31)
    lane = lax.rem(me_ref[0], C // capacity) * capacity + rank
    lanes = jnp.where(iota((C, points), 0) == lane, 1.0, 0.0).astype(bf16)
    nt = ((1,), (1,))
    high = mm(jnp.where(onehot, upper, 0).astype(f32).astype(bf16), lanes, nt)
    low = mm(jnp.where(onehot, lower, 0).astype(f32).astype(bf16), lanes, nt)
    ids = high * 32.0 + low
    out[:, capacity:, :] = jnp.broadcast_to(ids[:, None, :], (slabs, 8, C))


def weights_kernel(taps, backward):
    for i in range(3):
        for jk in range(9):
            high, low = split(taps[i * 9 + jk].T)
            columns = slice(jk * C, (jk + 1) * C)
            backward[i * C : (i + 1) * C, columns] = high
            backward[(3 + i) * C : (4 + i) * C, columns] = high
            backward[(6 + i) * C : (7 + i) * C, columns] = low


def split_taps(taps, forward):
    for i in range(3):
        for jk in range(9):
            high, low = split(taps[i * 9 + jk])
            for part in range(2):
                rows = slice(part * COLS + jk * C, part * COLS + (jk + 1) * C)
                forward[i, rows, :C] = high
                forward[i, rows, C:] = low


def codes_of(ids, chunk, group):
    total = ids[chunk * group]
    for t in range(1, group):
        total = total + ids[chunk * group + t]
    return total


def received(recv, capacity):
    slabs = recv.shape[0]
    rows = recv[:, :capacity, :].reshape(slabs * capacity, C)
    return recv[:, capacity:, :], jnp.concatenate(split(rows), axis=1)


def faces_kernel(capacity, lent, me, recv, to_core, to_far):
    group = C // capacity
    ids, row_parts = received(recv, capacity)
    row = iota((2 * FACE, C), 0)
    number = jnp.where(row < FACE, lent[0] * VOX + row, lent[1] * VOX + VOX - 2 * FACE + row)
    number = number.astype(f32) + 1.0
    hot = []
    for chunk in range(recv.shape[0] // group):
        match = number == codes_of(ids, chunk, group)[:1]
        hot.append(jnp.where(match, 1.0, 0.0).astype(bf16))
    sums = mm(jnp.concatenate(hot, axis=1), row_parts)
    sums = sums[:, :C] + sums[:, C:]
    even = jnp.bitwise_and(me[0], 1) == 0
    to_core[...] = jnp.where(even, sums[FACE:], sums[:FACE])
    to_far[...] = jnp.where(even, sums[:FACE], sums[FACE:])


def sublane(shape):
    return iota(shape, len(shape) - 2)


def plane_versions(first, center, last):
    three = [jnp.concatenate([first[k], center[k], last[k]], axis=0).reshape(PAD, E, C) for k in range(3)]
    z = sublane((PAD, E, C))
    down = pltpu.roll(jnp.where(z == E - 1, three[0], three[1]), 1, 1)
    up = pltpu.roll(jnp.where(z == 0, three[2], three[1]), E - 1, 1)
    return [v.reshape(PAD * E, C) for v in (down, three[1], up)]


def put_columns(columns, rows, versions):
    for k in range(3):
        for j in range(3):
            high, low = split(versions[k][E * j : E * j + FACE])
            at = (3 * j + k) * C
            columns[rows, at : at + C] = high
            columns[rows, COLS + at : COLS + at + C] = low


def load(source, block, stride, offset, size):
    return source[pl.ds(pl.multiple_of(block * stride + offset, E), size), :]


def build_plane(names, b, i, source, stride, offset, limit):
    def piece(j, k, at, size):
        name = jnp.minimum(names[b, 9 * i + 3 * j + k], limit)
        return load(source, name, stride, offset + at, size)

    first = [piece(0, k, FACE - E, E) for k in range(3)]
    center = [piece(1, k, 0, FACE) for k in range(3)]
    last = [piece(2, k, 0, E) for k in range(3)]
    return plane_versions(first, center, last)


def spread_plane(names, b, i, sums, target, stride, offset, limit):
    z = sublane((PAD, E, C))
    three = [s.reshape(PAD, E, C) for s in sums]
    down = pltpu.roll(three[0], E - 1, 1)
    up = pltpu.roll(three[2], 1, 1)
    zero = jnp.zeros_like(down)
    own = three[1] + jnp.where(z < E - 1, down, zero) + jnp.where(z > 0, up, zero)
    values = [jnp.where(z == E - 1, down, zero), own, jnp.where(z == 0, up, zero)]
    for k in range(3):
        value = values[k].reshape(PAD * E, C)
        for j, at, size, start in ((0, FACE - E, E, 0), (1, 0, FACE, E), (2, 0, E, E + FACE)):
            name = jnp.minimum(names[b, 9 * i + 3 * j + k], limit)
            where = pl.ds(pl.multiple_of(name * stride + offset + at, E), size)
            target[where, :] = target[where, :] + value[start : start + size]


def column_sums(back):
    sums = []
    for k in range(3):
        total = None
        for j in range(3):
            around = [back(3 * j + k)]
            if j > 0:
                around.insert(0, jnp.zeros((E * j, C), f32))
            if j < 2:
                around.append(jnp.zeros((E * (2 - j), C), f32))
            value = jnp.concatenate(around, axis=0)
            total = value if total is None else total + value
        sums.append(total)
    return sums


def interior_kernel(
    capacity, names_in, recv, taps_in,
    before, columns, faces, codes_out, forward,
    names, visible, taps, sems,
):
    names_copy = pltpu.make_async_copy(names_in, names, sems.at[0])
    taps_copy = pltpu.make_async_copy(taps_in, taps, sems.at[1])
    names_copy.start()
    taps_copy.start()
    voxels = NB * VOX
    group = C // capacity
    ids, row_parts = received(recv, capacity)
    tiles = []
    for chunk in range(recv.shape[0] // group):
        codes = codes_of(ids, chunk, group)
        codes_out[chunk * 8 : (chunk + 1) * 8, :] = codes
        tiles.append(codes[:1])
    for start in range(0, voxels, C):
        number = iota((C, C), 0).astype(f32) + (start + 1.0)
        hot = [jnp.where(number == tile, 1.0, 0.0).astype(bf16) for tile in tiles]
        sums = mm(jnp.concatenate(hot, axis=1), row_parts)
        visible[start : start + C] = sums[:, :C] + sums[:, C:]
    visible[voxels:] = jnp.zeros((VOX, C), f32)
    for b in range(NB):
        faces[b * FACE : (b + 1) * FACE] = visible[(b + 1) * VOX - FACE : (b + 1) * VOX]
        faces[(NB + b) * FACE : (NB + b + 1) * FACE] = visible[b * VOX : b * VOX + FACE]
    names_copy.wait()
    for b in range(NB):
        for x in range(E):
            rows = slice(b * VOX + x * FACE, b * VOX + (x + 1) * FACE)
            put_columns(columns, rows, build_plane(names, b, 1, visible, VOX, x * FACE, 2))
        if b == 0:
            taps_copy.wait()
            split_taps(taps, forward)
        low, high = b * VOX, (b + 1) * VOX
        total = mm(columns[low:high, :], forward[1])
        before[low:high] = total[:, :C] + total[:, C:]
        total = mm(columns[low : high - FACE, :], forward[0])
        before[low + FACE : high] = before[low + FACE : high] + total[:, :C] + total[:, C:]
        total = mm(columns[low + FACE : high, :], forward[2])
        before[low : high - FACE] = before[low : high - FACE] + total[:, :C] + total[:, C:]


def finish_kernel(
    names_in, me, before, faces, from_core, from_far, forward, backward, cotangent_in,
    activated_out, grads, outer, to_core, to_far,
    names, faces_low, faces_high, pre, cotangent, activated, edge_back, low_grads, high_grads, sems,
):
    copies = [
        pltpu.make_async_copy(names_in, names, sems.at[0]),
        pltpu.make_async_copy(cotangent_in, cotangent, sems.at[1]),
    ]
    for copy in copies:
        copy.start()
    even = jnp.bitwise_and(me[0], 1) == 0
    none = jnp.zeros((FACE, C), f32)
    faces_low[: 2 * FACE] = faces[: 2 * FACE]
    faces_low[2 * FACE : 3 * FACE] = jnp.where(even, from_far[...], from_core[...])
    faces_low[3 * FACE : 4 * FACE] = none
    faces_low[4 * FACE :] = none
    faces_high[: 2 * FACE] = faces[2 * FACE :]
    faces_high[2 * FACE : 3 * FACE] = none
    faces_high[3 * FACE : 4 * FACE] = jnp.where(even, from_core[...], from_far[...])
    faces_high[4 * FACE :] = none
    low_grads[...] = jnp.zeros_like(low_grads)
    high_grads[...] = jnp.zeros_like(high_grads)
    pre[...] = before[...]
    copies[0].wait()
    for n, (i, x, source) in enumerate(((0, 0, faces_low), (2, E - 1, faces_high))):
        for b in range(NB):
            rows = slice(b * FACE, (b + 1) * FACE)
            put_columns(outer.at[n], rows, build_plane(names, b, i, source, FACE, 0, 4))
        total = mm(outer[n], forward[i])
        total = total[:, :C] + total[:, C:]
        for b in range(NB):
            here = slice(b * VOX + x * FACE, b * VOX + (x + 1) * FACE)
            pre[here] = pre[here] + total[b * FACE : (b + 1) * FACE]
    value = pre[...]
    gate = jax.nn.sigmoid(value)
    activated[...] = value * gate
    copies.append(pltpu.make_async_copy(activated, activated_out, sems.at[2]))
    copies[2].start()
    copies[1].wait()
    high, low = split(cotangent[...] * gate * (1.0 + value * (1.0 - gate)))
    grads[:, :C] = high
    grads[:, C:] = low
    for n, (i, x, target) in enumerate(((0, 0, low_grads), (2, E - 1, high_grads))):
        both = jnp.concatenate([grads[b * VOX + x * FACE : b * VOX + (x + 1) * FACE, :] for b in range(NB)], axis=0)
        three = jnp.concatenate([both, both[:, :C]], axis=1)
        matching = jnp.concatenate([backward[(i + part) * C : (i + part + 1) * C, :] for part in (0, 3, 6)], axis=0)
        edge_back[...] = mm(three, matching)
        for b in range(NB):
            sums = column_sums(lambda jk: edge_back[b * FACE : (b + 1) * FACE, jk * C : (jk + 1) * C])
            spread_plane(names, b, i, sums, target, FACE, 0, 4)
    left = low_grads[2 * FACE : 3 * FACE]
    right = high_grads[3 * FACE : 4 * FACE]
    to_core[...] = jnp.where(even, right, left)
    to_far[...] = jnp.where(even, left, right)
    copies[2].wait()


def face_grads(grads, i):
    x = 0 if i == 0 else E - 1
    return jnp.concatenate([grads[(b * E + x) * FACE : (b * E + x + 1) * FACE, :] for b in range(NB)], axis=0)


def shifted_grads(grads, i):
    none = jnp.zeros((FACE, grads.shape[1]), bf16)
    rows = []
    for b in range(NB):
        block = grads[b * VOX : (b + 1) * VOX, :]
        rows += [[block[FACE:], none], [block], [none, block[: VOX - FACE]]][i]
    return jnp.concatenate(rows, axis=0)


def weight_grad_kernel(chunk, pieces, me, columns, outer, grads, kept_a, sent_a, kept_b, sent_b, ordered):
    tn = ((0,), (0,))
    shifted = [shifted_grads(grads, i) for i in range(3)]
    wide = jnp.concatenate(shifted, axis=1)
    narrow = jnp.concatenate([value[:, :C] for value in shifted], axis=1)
    faces = [face_grads(grads, i) for i in range(3)]
    for start in range(0, COLS, 3 * C):
        high = slice(start, start + 3 * C)
        low = slice(COLS + start, COLS + start + 3 * C)
        term = mm(columns[:, high], wide, tn)
        rest = mm(columns[:, low], narrow, tn)
        for i in range(3):
            value = term[:, 2 * i * C : (2 * i + 1) * C] + term[:, (2 * i + 1) * C : (2 * i + 2) * C]
            value = value + rest[:, i * C : (i + 1) * C]
            if i != 1:
                face = mm(outer[i // 2, :, high], faces[i], tn)
                value = value + face[:, :C] + face[:, C:]
                value = value + mm(outer[i // 2, :, low], faces[i][:, :C], tn)
            ordered[i * COLS + start : i * COLS + start + 3 * C] = value
    first = jnp.bitwise_and(me[0], 1) == 0
    for n, runs in enumerate(pieces):
        for (start, size, to), kept, sent in zip(runs, (kept_a, kept_b), (sent_a, sent_b)):
            start = 2 * n * chunk + start
            even = ordered[start : start + size]
            odd = ordered[start + chunk : start + chunk + size]
            kept[to : to + size] = jnp.where(first, even, odd)
            sent[to : to + size] = jnp.where(first, odd, even)


def halve_kernel(split_at, side, kept, arrived, kept_out, sent_out):
    total, half = kept.shape[0], kept_out.shape[0]
    for start, stop in ((0, split_at), (split_at, total)):
        size = (stop - start) // 2
        to = slice(start // 2, start // 2 + size)
        mine = pl.ds(pl.multiple_of(start + side[0] * size, 8), size)
        other = pl.ds(pl.multiple_of(start + (1 - side[0]) * size, 8), size)
        kept_out[to] = kept[mine, :] + arrived[mine, :]
        sent_out[to] = kept[other, :] + arrived[other, :]


def part_of(kept, arrived, start, size):
    return lax.dynamic_slice_in_dim(kept, start, size, 0) + lax.dynamic_slice_in_dim(arrived, start, size, 0)


def halve(kept, arrived, split_at, side):
    total = kept.shape[0]
    if split_at % 16 == 0 and total % 16 == 0:
        return pl.pallas_call(
            functools.partial(halve_kernel, split_at),
            out_shape=(struct(total // 2, C),) * 2,
            in_specs=[SMEM, VMEM, VMEM],
            out_specs=(VMEM, VMEM),
            compiler_params=params(4),
            name="halve",
            cost_estimate=cost(5),
        )(side.reshape(1), kept, arrived)
    one, two = split_at // 2, (total - split_at) // 2

    def take(which):
        return jnp.concatenate(
            [part_of(kept, arrived, which * one, one), part_of(kept, arrived, split_at + which * two, two)], axis=0
        )

    return take(side), take(1 - side)


def backward_kernel(
    names_in, lent, me, grads, backward, halo_core, halo_far, blocks_out,
    names, shifted, back, target, sem,
):
    names_copy = pltpu.make_async_copy(names_in, names, sem)
    names_copy.start()
    target[...] = jnp.zeros_like(target)
    shifted[...] = jnp.zeros_like(shifted)
    for b in range(NB):
        rows = slice(b * VOX, (b + 1) * VOX)
        for i in range(3):
            at = slice(FACE * i, FACE * i + VOX)
            shifted[at, i * C : (i + 1) * C] = grads[rows, :C]
            shifted[at, (3 + i) * C : (4 + i) * C] = grads[rows, C:]
            shifted[at, (6 + i) * C : (7 + i) * C] = grads[rows, :C]
        back[b] = mm(shifted[...], backward[...])
    names_copy.wait()
    for b in range(NB):
        for p in range(PAD):
            i = 0 if p == 0 else 2 if p == PAD - 1 else 1
            offset = (VOX - FACE, (p - 1) * FACE, 0)[i]
            rows = slice(p * FACE, (p + 1) * FACE)
            sums = column_sums(lambda jk: back[b, rows, jk * C : (jk + 1) * C])
            spread_plane(names, b, i, sums, target, VOX, offset, 2)
    even = jnp.bitwise_and(me[0], 1) == 0
    left = pl.ds(pl.multiple_of(lent[0] * VOX, VOX), FACE)
    right = pl.ds(pl.multiple_of(lent[1] * VOX, VOX) + VOX - FACE, FACE)
    target[left, :] = target[left, :] + jnp.where(even, halo_far[...], halo_core[...])
    target[right, :] = target[right, :] + jnp.where(even, halo_core[...], halo_far[...])
    blocks_out[...] = target[: NB * VOX]


def gather_kernel(grad_blocks, codes, out):
    voxels = NB * VOX
    parts = jnp.concatenate(split(grad_blocks[...]), axis=1)
    by_row = codes[...].T
    numbers = iota((C, voxels), 1).astype(f32) + 1.0
    for chunk in range(codes.shape[0] // 8):
        match = numbers == by_row[:, chunk * 8 : chunk * 8 + 1]
        rows = mm(jnp.where(match, 1.0, 0.0).astype(bf16), parts)
        out[chunk * C : (chunk + 1) * C] = rows[:, :C] + rows[:, C:]


def pass_kernel(rows, one, two, out):
    del rows, one, two, out


def unpack_kernel(came_back, dest, out):
    places = dest[...].astype(f32).T[:, :1]
    points, slots = out.shape[0], came_back.shape[0]
    chosen = jnp.where(iota((points, slots), 1).astype(f32) == places, 1.0, 0.0).astype(bf16)
    rows = mm(chosen, jnp.concatenate(split(came_back[...]), axis=1))
    out[...] = rows[:, :C] + rows[:, C:]


def place(slab, order):
    number = 0
    for bit in order:
        number = 2 * number + (slab >> bit & 1)
    return number


def per_device(
    point_feats, owner_slab, block_slot, voxel_index, boundary, neighbours, weight_taps, cotangent
):
    slabs = lax.axis_size("slab")
    windows = lax.axis_size("dp")
    points = point_feats.shape[1]
    capacity = 2 * points // slabs
    bits = slabs.bit_length() - 1
    me = lax.axis_index("slab")
    names = neighbours[0]
    lent = boundary.reshape(2)
    voxels = NB * VOX
    chunk = 27 * C // slabs

    send, dest = pl.pallas_call(
        functools.partial(pack_kernel, slabs, capacity),
        out_shape=(struct(slabs, capacity + 8, C), struct(8, points, dtype=jnp.int32)),
        in_specs=[SMEM] + [HBM] * 4,
        out_specs=(VMEM, VMEM),
        scratch_shapes=[pltpu.VMEM((points, C), f32)]
        + [pltpu.VMEM((1, points), jnp.int32)] * 3
        + [pltpu.SemaphoreType.DMA((4,))],
        compiler_params=params(60),
        name="pack",
        cost_estimate=cost(2),
    )(me.reshape(1), point_feats[0], owner_slab.reshape(1, points), block_slot, voxel_index)
    send, weight_taps = lax.optimization_barrier((send, weight_taps))
    recv = lax.all_to_all(send, "slab", split_axis=0, concat_axis=0, tiled=True)
    backward = pl.pallas_call(
        weights_kernel,
        out_shape=struct(9 * C, COLS, dtype=bf16),
        in_specs=[VMEM],
        out_specs=VMEM,
        compiler_params=params(4),
        name="weights",
        cost_estimate=cost(0.6),
    )(weight_taps)
    recv, backward = lax.optimization_barrier((recv, backward))
    to_core, to_far = pl.pallas_call(
        functools.partial(faces_kernel, capacity),
        out_shape=(struct(FACE, C), struct(FACE, C)),
        in_specs=[SMEM, SMEM, VMEM],
        out_specs=(VMEM,) * 2,
        compiler_params=params(8),
        name="faces",
        cost_estimate=cost(0.8),
    )(lent, me.reshape(1), recv)
    core_pairs = [(i, i ^ 1) for i in range(slabs)]
    far_pairs = [(i, (i - 1 if i % 2 == 0 else i + 1) % slabs) for i in range(slabs)]
    from_core = lax.ppermute(to_core, "slab", core_pairs)
    from_far = lax.ppermute(to_far, "slab", far_pairs)
    before, columns, faces, codes, forward = pl.pallas_call(
        functools.partial(interior_kernel, capacity),
        out_shape=(
            struct(voxels, C),
            struct(voxels, 2 * COLS, dtype=bf16),
            struct(2 * NB * FACE, C),
            struct(slabs * capacity // C * 8, C),
            struct(3, 2 * COLS, 2 * C, dtype=bf16),
        ),
        in_specs=[ANY, VMEM, ANY],
        out_specs=(VMEM,) * 5,
        scratch_shapes=[
            pltpu.SMEM((NB, 27), jnp.int32),
            pltpu.VMEM((3 * VOX, C), f32),
            pltpu.VMEM(weight_taps.shape, f32),
            pltpu.SemaphoreType.DMA((2,)),
        ],
        compiler_params=params(16),
        name="interior",
        cost_estimate=cost(5),
    )(names, recv, weight_taps)
    activated, grads, outer, edge_core, edge_far = pl.pallas_call(
        finish_kernel,
        out_shape=(
            struct(voxels, C),
            struct(voxels, 2 * C, dtype=bf16),
            struct(2, NB * FACE, 2 * COLS, dtype=bf16),
            struct(FACE, C),
            struct(FACE, C),
        ),
        in_specs=[ANY, SMEM] + [VMEM] * 6 + [ANY],
        out_specs=(ANY,) + (VMEM,) * 4,
        scratch_shapes=[
            pltpu.SMEM((NB, 27), jnp.int32),
            pltpu.VMEM((5 * FACE, C), f32),
            pltpu.VMEM((5 * FACE, C), f32),
            pltpu.VMEM((voxels, C), f32),
            pltpu.VMEM((voxels, C), f32),
            pltpu.VMEM((voxels, C), f32),
            pltpu.VMEM((NB * FACE, COLS), f32),
            pltpu.VMEM((5 * FACE, C), f32),
            pltpu.VMEM((5 * FACE, C), f32),
            pltpu.SemaphoreType.DMA((3,)),
        ],
        compiler_params=params(14),
        name="finish",
        cost_estimate=cost(2.8),
    )(names, me.reshape(1), before, faces, from_core, from_far, forward, backward, cotangent[0])
    cut = -(-chunk // 16) * 8
    rest = list(range(3, bits))
    orders = ([1, 2] + rest, [2, 1] + rest)
    pieces = tuple(
        (
            (0, cut, place(2 * n, orders[0]) * cut),
            (cut, chunk - cut, place(2 * n, orders[1]) * (chunk - cut)),
        )
        for n in range(slabs // 2)
    )
    sizes = (slabs // 2 * cut, slabs // 2 * (chunk - cut))
    kept_a, sent_a, kept_b, sent_b = pl.pallas_call(
        functools.partial(weight_grad_kernel, chunk, pieces),
        out_shape=(struct(sizes[0], C),) * 2 + (struct(sizes[1], C),) * 2,
        in_specs=[SMEM] + [VMEM] * 3,
        out_specs=(VMEM,) * 4,
        scratch_shapes=[pltpu.VMEM((27 * C, C), f32)],
        compiler_params=params(9),
        name="weight_grad",
        cost_estimate=cost(4),
    )(me.reshape(1), columns, outer, grads)
    def swapped(part, axis, bit):
        size = lax.axis_size(axis)
        return lax.ppermute(part, axis, [(i, i ^ (1 << bit)) for i in range(size)])

    def side(bit):
        return lax.shift_right_logical(me, bit) & 1

    halo_far = lax.ppermute(edge_far, "slab", far_pairs)
    halo_core = lax.ppermute(edge_core, "slab", core_pairs)
    kept, arrived = (kept_a, kept_b), (swapped(sent_a, "slab", 0), swapped(sent_b, "slab", 0))
    sides, halves = (side(1), side(2)), [size // 2 for size in sizes]
    sent = [part_of(kept[q], arrived[q], (1 - sides[q]) * halves[q], halves[q]) for q in range(2)]
    sent[0], sent[1], grads = lax.optimization_barrier((sent[0], sent[1], grads))
    kept = [part_of(kept[q], arrived[q], sides[q] * halves[q], halves[q]) for q in range(2)]
    arrived = [swapped(sent[q], "slab", (1, 2)[q]) for q in range(2)]
    grad_blocks = pl.pallas_call(
        backward_kernel,
        out_shape=struct(voxels, C),
        in_specs=[ANY, SMEM, SMEM] + [VMEM] * 4,
        out_specs=VMEM,
        scratch_shapes=[
            pltpu.SMEM((NB, 27), jnp.int32),
            pltpu.VMEM((PAD * FACE, 9 * C), bf16),
            pltpu.VMEM((NB, PAD * FACE, COLS), f32),
            pltpu.VMEM((3 * VOX, C), f32),
            pltpu.SemaphoreType.DMA,
        ],
        compiler_params=params(14),
        name="backward",
        cost_estimate=cost(6.5),
    )(names, lent, me.reshape(1), grads, backward, halo_core, halo_far)
    back_points = pl.pallas_call(
        gather_kernel,
        out_shape=struct(slabs * capacity, C),
        in_specs=[VMEM, VMEM],
        out_specs=VMEM,
        compiler_params=params(12),
        name="gather",
        cost_estimate=cost(2.2),
    )(grad_blocks, codes)
    arrived[0], arrived[1], back_points = lax.optimization_barrier((arrived[0], arrived[1], back_points))
    sides, halves = (side(2), side(1)), [half // 2 for half in halves]
    sent = [part_of(kept[q], arrived[q], (1 - sides[q]) * halves[q], halves[q]) for q in range(2)]
    kept = [part_of(kept[q], arrived[q], sides[q] * halves[q], halves[q]) for q in range(2)]
    back_points = pl.pallas_call(
        pass_kernel,
        out_shape=struct(slabs * capacity, C),
        in_specs=[ANY] * 3,
        out_specs=ANY,
        input_output_aliases={0: 0},
        name="pass",
        cost_estimate=cost(2.2),
    )(back_points, *sent)
    arrived = [swapped(sent[q], "slab", (2, 1)[q]) for q in range(2)]
    came_back = lax.all_to_all(
        back_points.reshape(slabs, capacity, C), "slab", split_axis=0, concat_axis=0, tiled=True
    )
    point_grads = pl.pallas_call(
        unpack_kernel,
        out_shape=struct(points, C),
        in_specs=[VMEM, VMEM],
        out_specs=VMEM,
        compiler_params=params(12),
        name="unpack",
        cost_estimate=cost(1.7),
    )(came_back.reshape(slabs * capacity, C), dest)

    kept = jnp.concatenate([kept[q] + arrived[q] for q in range(2)], axis=0)
    split_at, step = halves[0], 0
    while (1 << step) < windows:
        arrived = swapped(kept, "dp", step)
        step += 1
        if (1 << step) < windows:
            kept = kept + arrived
    for bit in rest:
        kept, sent = halve(kept, arrived, split_at, side(bit))
        arrived = swapped(sent, "slab", bit)
        split_at //= 2
    arrived, point_grads = lax.optimization_barrier((arrived, point_grads))
    share = kept + arrived
    scale = 1.0 / math.sqrt(windows * slabs * voxels)
    return (activated[None], point_grads[None], share * scale)


def solution(mesh):
    return jax.shard_map(
        per_device,
        mesh=mesh,
        in_specs=(
            P("dp", "slab", None),
            P("dp", "slab", None),
            P("dp", "slab"),
            P("dp", "slab"),
            P("dp", "slab", None, None),
            P("dp", "slab", None),
            P(),
            P("dp", "slab", None),
        ),
        out_specs=(P("dp", "slab", None), P("dp", "slab", None), P("slab", None)),
        check_vma=False,
    )
```
